128 devices in a mesh: off: 16 (over x, y), col: 8 (over z, core).
Axes of the slice: x: 4, y: 4, z: 4, core: 2. Of those that a mesh axis runs over, the one named last changes fastest.
Arguments:
- noise_cov: float32 [512, 256, 256], P('off', 'col'), as said below
- couplings: float32 [3, 256, 256], replicated, may hold values from -0.3125 to 0.3125
- shifts: int32 [3], replicated, may hold values from -1 to 1
Outputs:
- covariance: float32 [512, 256, 256], P('off', 'col')
The draws below stay inside these ranges and needn't reach their ends.
Inputs may be any that keep to these rules, and one draw needn't show every extreme that they name: noise_cov[d] is the transpose of noise_cov[(512 - d) mod 512].
All inputs are finite; a program needn't handle non-finite values.
Results may differ from the reference program's by a relative error of at most 0.0003.
Values sent between devices are 32-bit elements; how exact they have to be, the bound alone decides.
No kernel may reach another device: no remote copies, remote signals or barrier semaphores. Data moves between devices by JAX's collectives and lax.ppermute only.
A program may use at most 64 MiB of HBM per device.

```python
import math
import jax
import jax.numpy as jnp
from jax import lax

CELLS = 512
N_STATE = 256
TERMS = 3


def draw_noise_cov(key, part):
    key = jax.random.fold_in(key, 11)
    base = jax.random.normal(key, (CELLS, N_STATE, N_STATE), jnp.float32)
    mirrored = jnp.roll(jnp.flip(base, 0), 1, 0)
    blocks = (base + jnp.swapaxes(mirrored, 1, 2)) * 0.7071
    return blocks


def gaussian(rng, extent, spread, most, kind=jnp.bfloat16):
    entries = jax.random.normal(rng, extent, jnp.float32) * spread
    return jnp.minimum(jnp.maximum(entries, -most), most).astype(kind)


def setup_inputs(seed: int = 0) -> dict:
    arg_keys = jax.random.split(jax.random.key(seed), 4)
    return {
        "noise_cov": draw_noise_cov(jax.random.fold_in(arg_keys[3], 71), 0),
        "couplings": gaussian(arg_keys[1], (TERMS, N_STATE, N_STATE), 0.022, 0.3125, jnp.float32),
        "shifts": jax.random.randint(arg_keys[2], (TERMS,), -1, 2).astype(jnp.int32),
    }


highest = lax.Precision.HIGHEST


def angle_table(count):
    index = jnp.arange(count, dtype=jnp.int32)
    product = (index[:, None] * index[None, :]) % count
    return (2.0 * math.pi / count) * product.astype(jnp.float32)


def coupling(waves, couplings, shifts, count):
    phase = (2.0 * math.pi / count) * ((waves[:, None] * shifts[None, :]) % count).astype(jnp.float32)
    map_real = jnp.einsum('kt,tij->kij', jnp.cos(phase), couplings, precision=highest)
    map_imag = -jnp.einsum('kt,tij->kij', jnp.sin(phase), couplings, precision=highest)
    return map_real, map_imag


def sandwich(cov_real, cov_imag, map_real, map_imag):
    left_real = jnp.einsum('kri,kji->krj', cov_real, map_real, precision=highest) + jnp.einsum('kri,kji->krj', cov_imag, map_imag, precision=highest)
    left_imag = jnp.einsum('kri,kji->krj', cov_imag, map_real, precision=highest) - jnp.einsum('kri,kji->krj', cov_real, map_imag, precision=highest)
    outer_real = jnp.einsum('kri,kij->krj', map_real, left_real, precision=highest) - jnp.einsum('kri,kij->krj', map_imag, left_imag, precision=highest)
    outer_imag = jnp.einsum('kri,kij->krj', map_real, left_imag, precision=highest) + jnp.einsum('kri,kij->krj', map_imag, left_real, precision=highest)
    return cov_real + outer_real, cov_imag + outer_imag


def doubling(cov_real, cov_imag, waves, couplings, shifts, count):
    map_real, map_imag = coupling(waves, couplings, shifts, count)
    cov_real, cov_imag = sandwich(cov_real, cov_imag, map_real, map_imag)
    square_real = jnp.einsum('kij,kjl->kil', map_real, map_real, precision=highest) - jnp.einsum('kij,kjl->kil', map_imag, map_imag, precision=highest)
    square_imag = jnp.einsum('kij,kjl->kil', map_real, map_imag, precision=highest) + jnp.einsum('kij,kjl->kil', map_imag, map_real, precision=highest)
    return sandwich(cov_real, cov_imag, square_real, square_imag)


def reference(noise_cov, couplings, shifts):
    angles = angle_table(CELLS)
    cosine = jnp.cos(angles)
    sine = jnp.sin(angles)
    flat = noise_cov.reshape(CELLS, N_STATE * N_STATE)
    wave_real = jnp.dot(cosine, flat, precision=highest).reshape(CELLS // 8, 8, N_STATE, N_STATE)
    wave_imag = (-jnp.dot(sine, flat, precision=highest)).reshape(CELLS // 8, 8, N_STATE, N_STATE)
    waves = jnp.arange(CELLS, dtype=jnp.int32).reshape(CELLS // 8, 8)

    def block_step(items):
        return doubling(items[0], items[1], items[2], couplings, shifts, CELLS)

    doubled_real, doubled_imag = lax.map(block_step, (wave_real, wave_imag, waves))
    result = jnp.dot(cosine, doubled_real.reshape(CELLS, N_STATE * N_STATE), precision=highest)
    result = result - jnp.dot(sine, doubled_imag.reshape(CELLS, N_STATE * N_STATE), precision=highest)
    return (result / CELLS).reshape(CELLS, N_STATE, N_STATE)
```

```python
import functools

import jax
import jax.numpy as jnp
from jax import lax
from jax.experimental import pallas as pl
from jax.experimental.pallas import tpu as pltpu
from jax.sharding import PartitionSpec as P

f32 = jnp.float32
bf16 = jnp.bfloat16

N = 256
R = 32
HALO = 6
GRID = 6
BASE = 3

NEED = {3: range(-3, 20), 2: range(-2, 19), 1: range(-1, 18)}


def place(d):
    slot = d + BASE
    return slot % GRID, slot // GRID


def message_tiles():
    tiles = []
    for j in (3, 2, 1):
        for g in range(GRID):
            entries = []
            for q in range(4):
                d = GRID * q + g - BASE
                entries.append((j, d) if d in NEED[j] else None)
            tiles.append(entries)
    return tiles


TILES = message_tiles()
LANES = 128 * len(TILES)
RESULT = [[5, 3, 9, 15], [11, 4, 10, 16], [0, 6, 12, None], [1, 7, 13, None], [2, 8, 14, None]]
OUT_LANES = 128 * len(RESULT)
SLOTS = [(k, e) for k in range(4) for e in range(2)]


def coordinates():
    col = lax.axis_index("col")
    return col // 2, col % 2


def target(k, e):
    z, core = coordinates()
    return 2 * ((z + k) % 4) + (core + e) % 2


def source(k, e):
    z, core = coordinates()
    return 2 * ((z + 4 - k) % 4) + (core + e) % 2


def split(x):
    high = x.astype(bf16)
    return high, (x - high.astype(f32)).astype(bf16)


def taps(c_ref, shift_ref):
    blocks = []
    for s in (-1, 0, 1):
        block = None
        for t in range(3):
            chosen = jnp.where(shift_ref[t] == s, f32(1), f32(0)) * c_ref[t]
            block = chosen if block is None else block + chosen
        blocks.append(block)
    return blocks


def block_of_lane(rows):
    return lax.broadcasted_iota(jnp.int32, (rows, 128), 1) // 32


def exchange_blocks(tiles):
    block = block_of_lane(tiles[0].shape[0])
    low = block < 2
    even = block % 2 == 0
    a = list(tiles)
    for q in (0, 1):
        x, y = a[q], a[q + 2]
        a[q] = jnp.where(low, x, pltpu.roll(y, 64, 1))
        a[q + 2] = jnp.where(low, pltpu.roll(x, 64, 1), y)
    for q in (0, 2):
        x, y = a[q], a[q + 1]
        a[q] = jnp.where(even, x, pltpu.roll(y, 32, 1))
        a[q + 1] = jnp.where(even, pltpu.roll(x, 96, 1), y)
    return a


def nt(x, y):
    return lax.dot_general(x, y, (((1,), (1,)), ((), ())), preferred_element_type=f32)


def nn(x, y):
    return lax.dot_general(x, y, (((1,), (0,)), ((), ())), preferred_element_type=f32)


def right_kernel(shift_ref, n_ref, halo_ref, c_ref, *rest):
    outs = rest[:8]
    x_scr, b_scr, v_scr, m_scr = rest[8:]
    for s, block in enumerate(taps(c_ref, shift_ref)):
        high, low = split(block)
        b_scr[s, :, :N] = high
        b_scr[s, :, N:] = low
    halo = halo_ref[...].reshape(HALO * R, N)
    own = n_ref[0:23].reshape(23 * R, N)
    x = jnp.concatenate([halo, own], axis=0)
    first = -HALO
    count = 29
    start = {}
    for j in (1, 2, 3):
        high, low = split(x)
        x_scr[: count * R, :N] = high
        x_scr[: count * R, N:] = low
        count -= 2
        first += 1
        total = None
        for s in range(3):
            rows = pl.ds(s * R, count * R)
            bh, bl = b_scr[s, :, :N], b_scr[s, :, N:]
            part = nt(x_scr[rows, :N], bh) + nt(x_scr[rows, N:], bh) + nt(x_scr[rows, :N], bl)
            total = part if total is None else total + part
        x = total
        v_scr[j - 1, : count * R] = x
        start[j] = first
    for m, entries in enumerate(TILES):
        filler = next(entry for entry in entries if entry is not None)
        for h in range(2):
            parts = []
            for entry in entries:
                j, d = entry or filler
                row = (d - start[j]) * R
                parts.append(v_scr[j - 1, row : row + R, 128 * h : 128 * (h + 1)])
            for b, part in enumerate(exchange_blocks(parts)):
                m_scr[4 * h + b, :, 128 * m : 128 * (m + 1)] = part
    for out, slot in zip(outs, SLOTS):
        out[...] = m_scr[target(*slot)]


def left_kernel(shift_ref, c_ref, *rest):
    received = rest[:8]
    outs = rest[8:16]
    mirror_ref = rest[16]
    b_scr, r_scr, x_scr, f_scr = rest[17:]
    for s, block in enumerate(taps(c_ref, shift_ref)):
        high, low = split(block)
        b_scr[s, :, :N] = high
        b_scr[s, :, N:] = low
    for ref, slot in zip(received, SLOTS):
        row = pl.multiple_of(source(*slot) * R, R)
        r_scr[pl.ds(row, R), :] = ref[...]
    total = None
    for step, j in enumerate((3, 2, 1)):
        x = r_scr[:, 128 * GRID * step : 128 * GRID * (step + 1)]
        if total is not None:
            x = x + total
        before = pltpu.roll(x[:, 128 * (GRID - 1) :], 32, 1)
        after = pltpu.roll(x[:, :128], 96, 1)
        for lane, part in ((0, before), (128, x), (128 * (GRID + 1), after)):
            high, low = split(part)
            x_scr[:N, lane : lane + part.shape[1]] = high
            x_scr[N:, lane : lane + part.shape[1]] = low
        total = None
        for s in range(3):
            lanes = pl.ds(128 * (2 - s), 128 * GRID)
            bh, bl = b_scr[s, :, :N], b_scr[s, :, N:]
            part = nn(bh, x_scr[:N, lanes]) + nn(bh, x_scr[N:, lanes]) + nn(bl, x_scr[:N, lanes])
            total = part if total is None else total + part
    tiles = [total[:, 128 * g : 128 * (g + 1)] for g in range(GRID)]
    block = block_of_lane(N)
    for m, entries in enumerate(RESULT):
        value = None
        for q, d in enumerate(entries):
            if d is None:
                continue
            g, p = place(d)
            part = tiles[g] if p == q else pltpu.roll(tiles[g], (32 * (q - p)) % 128, 1)
            value = part if value is None else jnp.where(block == q, part, value)
        f_scr[:, 128 * m : 128 * (m + 1)] = value
    for out, slot in zip(outs, SLOTS):
        row = pl.multiple_of(target(*slot) * R, R)
        out[...] = f_scr[pl.ds(row, R), :]
    for g in range(GRID):
        turned = tiles[g].T
        for q in range(4):
            d = GRID * q + g - BASE
            if 1 <= d <= 15:
                mirror_ref[15 - d] = turned[32 * q : 32 * (q + 1)]


def join_kernel(n_ref, mirror_ref, *rest):
    received = rest[:8]
    out_ref, r_scr = rest[8:]
    for ref, slot in zip(received, SLOTS):
        r_scr[source(*slot)] = ref[...]
    for m, entries in enumerate(RESULT):
        for h in range(2):
            lanes = slice(128 * h, 128 * (h + 1))
            parts = [r_scr[4 * h + b, :, 128 * m : 128 * (m + 1)] for b in range(4)]
            for d, part in zip(entries, exchange_blocks(parts)):
                if d is not None:
                    out_ref[d, :, lanes] = n_ref[d, :, lanes] + part
    out_ref[17:] = n_ref[17:] + mirror_ref[...]


PARAMS = pltpu.CompilerParams(vmem_limit_bytes=48 * 1024 * 1024)
SMEM = pl.BlockSpec(memory_space=pltpu.SMEM)
VMEM = pl.BlockSpec(memory_space=pltpu.VMEM)


def spread(arrays):
    moved = []
    for array, (k, e) in zip(arrays, SLOTS):
        if (k, e) == (0, 0):
            moved.append(array)
        else:
            pairs = [(c, 2 * ((c // 2 + k) % 4) + (c + e) % 2) for c in range(8)]
            moved.append(lax.ppermute(array, "col", pairs))
    return moved


def body(noise_cov, couplings, shifts):
    halo = lax.ppermute(noise_cov[R - HALO :], "off", [(o, (o + 1) % 16) for o in range(16)])
    messages = pl.pallas_call(
        right_kernel,
        out_shape=[jax.ShapeDtypeStruct((R, LANES), f32)] * 8,
        in_specs=[SMEM, VMEM, VMEM, VMEM],
        out_specs=[VMEM] * 8,
        scratch_shapes=[
            pltpu.VMEM((29 * R, 2 * N), bf16),
            pltpu.VMEM((3, N, 2 * N), bf16),
            pltpu.VMEM((3, 27 * R, N), f32),
            pltpu.VMEM((8, R, LANES), f32),
        ],
        compiler_params=PARAMS,
        name="right_products",
    )(shifts, noise_cov, halo, couplings)
    received = spread(messages)
    *rows, mirror = pl.pallas_call(
        left_kernel,
        out_shape=[jax.ShapeDtypeStruct((R, OUT_LANES), f32)] * 8 + [jax.ShapeDtypeStruct((15, R, N), f32)],
        in_specs=[SMEM, VMEM] + [VMEM] * 8,
        out_specs=[VMEM] * 9,
        scratch_shapes=[
            pltpu.VMEM((3, N, 2 * N), bf16),
            pltpu.VMEM((N, LANES), f32),
            pltpu.VMEM((2 * N, 128 * (GRID + 2)), bf16),
            pltpu.VMEM((N, OUT_LANES), f32),
        ],
        compiler_params=PARAMS,
        name="left_products",
    )(shifts, couplings, *received)
    mirror = lax.ppermute(mirror, "off", [(o, 15 - o) for o in range(16)])
    rows = spread(rows)
    return pl.pallas_call(
        join_kernel,
        out_shape=jax.ShapeDtypeStruct((R, R, N), f32),
        in_specs=[VMEM] * 10,
        out_specs=VMEM,
        scratch_shapes=[pltpu.VMEM((8, R, OUT_LANES), f32)],
        compiler_params=PARAMS,
        name="join",
    )(noise_cov, mirror, *rows)


def solution(mesh):
    return jax.shard_map(
        body,
        mesh=mesh,
        in_specs=(P("off", "col", None), P(), P()),
        out_specs=P("off", "col", None),
        check_vma=False,
    )
```

```python
import jax
import jax.numpy as jnp
from jax import lax
from jax.experimental import pallas as pl
from jax.experimental.pallas import tpu as pltpu
from jax.sharding import PartitionSpec as P

f32 = jnp.float32
bf16 = jnp.bfloat16

N = 256
R = 32
HALO = 6
GRID = 6
BASE = 3

def place(d):
    slot = d + BASE
    return slot % GRID, slot // GRID


def grid_tile(j, g, offsets):
    return [(j, GRID * q + g - BASE) if GRID * q + g - BASE in offsets else None for q in range(4)]


def local_tiles():
    tiles = [grid_tile(3, g, range(3, 20)) for g in range(GRID)]
    tiles += [grid_tile(2, g, range(2, 19)) for g in range(GRID)]
    tiles += [grid_tile(1, 5, range(1, 18))]
    free = [(tile, q) for tile in tiles[:-1] for q in range(4) if tile[q] is None]
    left = [d for d in range(1, 18) if place(d)[0] != 5]
    for tile, q in [f for f in free if f[1] == 3]:
        d = next(d for d in left if place(d)[1] == 3)
        left.remove(d)
        tile[q] = (1, d)
        free.remove((tile, q))
    for (tile, q), d in zip(free, left):
        tile[q] = (1, d)
    return tiles


LOCAL = local_tiles()
HALOS = [
    [(3, -3), (3, -2), (3, -1), (3, 0)],
    [(3, 1), (3, 2), (2, -2), (2, -1)],
    [(2, 0), (2, 1), (1, -1), (1, 0)],
]
WHERE = {entry: (m, p) for m, tile in enumerate(LOCAL + HALOS) for p, entry in enumerate(tile) if entry}
RESULT = [[5, 3, 9, 15], [11, 4, 10, 16], [0, 6, 12, None], [1, 7, 13, None], [2, 8, 14, None]]
LOCAL_LANES = 128 * len(LOCAL)
HALO_LANES = 128 * len(HALOS)
OUT_LANES = 128 * len(RESULT)
SLOTS = [(1, 0), (3, 0), (2, 0), (1, 1), (3, 1), (2, 1), (0, 1), (0, 0)]


def coordinates():
    col = lax.axis_index("col")
    return col // 2, col % 2


def target(k, e):
    z, core = coordinates()
    return 2 * ((z + k) % 4) + (core + e) % 2


def source(k, e):
    z, core = coordinates()
    return 2 * ((z + 4 - k) % 4) + (core + e) % 2


def split(x):
    high = x.astype(bf16)
    return high, (x - high.astype(f32)).astype(bf16)


def split_taps(c_ref, shift_ref, b_ref):
    for s in (-1, 0, 1):
        block = None
        for t in range(3):
            chosen = jnp.where(shift_ref[t] == s, f32(1), f32(0)) * c_ref[t]
            block = chosen if block is None else block + chosen
        high, low = split(block)
        b_ref[s + 1, :, :N] = high
        b_ref[s + 1, :, N : 2 * N] = high
        b_ref[s + 1, :, 2 * N :] = low


def block_of_lane(rows):
    return lax.broadcasted_iota(jnp.int32, (rows, 128), 1) // 32


def exchange_blocks(tiles):
    block = block_of_lane(tiles[0].shape[0])
    low = block < 2
    even = block % 2 == 0
    a = list(tiles)
    for q in (0, 1):
        x, y = a[q], a[q + 2]
        a[q] = jnp.where(low, x, pltpu.roll(y, 64, 1))
        a[q + 2] = jnp.where(low, pltpu.roll(x, 64, 1), y)
    for q in (0, 2):
        x, y = a[q], a[q + 1]
        a[q] = jnp.where(even, x, pltpu.roll(y, 32, 1))
        a[q + 1] = jnp.where(even, pltpu.roll(x, 96, 1), y)
    return a


def nt(x, y):
    return lax.dot_general(x, y, (((1,), (1,)), ((), ())), preferred_element_type=f32)


def nn(x, y):
    return lax.dot_general(x, y, (((1,), (0,)), ((), ())), preferred_element_type=f32)


def right_products(x, first, tiles, b_scr, x_scr, v_scr, m_ref):
    count = x.shape[0] // R
    start = {}
    for j in (1, 2, 3):
        high, low = split(x)
        x_scr[: count * R, :N] = high
        x_scr[: count * R, N : 2 * N] = low
        x_scr[: count * R, 2 * N :] = high
        count -= 2
        first += 1
        total = None
        for s in range(3):
            part = nt(x_scr[s * R : (s + count) * R], b_scr[s])
            total = part if total is None else total + part
        x = total
        v_scr[j - 1, : count * R] = x
        start[j] = first
    for m, entries in enumerate(tiles):
        filler = next(entry for entry in entries if entry is not None)
        for h in range(2):
            parts = []
            for entry in entries:
                j, d = entry or filler
                row = (d - start[j]) * R
                parts.append(v_scr[j - 1, row : row + R, 128 * h : 128 * (h + 1)])
            for b, part in enumerate(exchange_blocks(parts)):
                m_ref[4 * h + b, :, 128 * m : 128 * (m + 1)] = part


def local_kernel(shift_ref, n_ref, c_ref, *rest):
    outs = rest[:8]
    edge_ref, first_ref, b_ref, x_scr, v_scr, m_scr = rest[8:]
    edge_ref[...] = n_ref[R - HALO :]
    first_ref[...] = n_ref[:HALO]
    split_taps(c_ref, shift_ref, b_ref)
    right_products(n_ref[0:23].reshape(23 * R, N), 0, LOCAL, b_ref, x_scr, v_scr, m_scr)
    for out, slot in zip(outs, SLOTS):
        out[...] = m_scr[target(*slot)]


def halo_kernel(halo_ref, first_ref, b_ref, *rest):
    outs = rest[:4]
    x_scr, v_scr, m_scr = rest[4:]
    x = jnp.concatenate([halo_ref[...].reshape(HALO * R, N), first_ref[...].reshape(HALO * R, N)], axis=0)
    right_products(x, -HALO, HALOS, b_ref, x_scr, v_scr, m_scr)
    for k, out in enumerate(outs):
        for e in range(2):
            out[e] = m_scr[target(k, e)]


def gather_kernel(*refs):
    for ref, slot in zip(refs, SLOTS):
        row = pl.multiple_of(source(*slot) * R, R)
        refs[8][pl.ds(row, R), :] = ref[...]


def left_kernel(b_ref, r_ref, *rest):
    received = rest[:4]
    other_ref, result_ref, mirror_ref, x_scr, h_scr = rest[4:]
    for k, ref in enumerate(received):
        h_scr[pl.ds(pl.multiple_of(source(k, 0) * R, R), R), :] = ref[0]
        h_scr[pl.ds(pl.multiple_of(source(k, 1) * R, R), R), :] = other_ref[k]
    block = block_of_lane(N)
    total = None
    for j in (3, 2, 1):
        tiles = []
        for g in range(GRID):
            value = None
            for q in range(4):
                entry = (j, GRID * q + g - BASE)
                if entry not in WHERE:
                    continue
                m, p = WHERE[entry]
                if m < len(LOCAL):
                    part = r_ref[:, 128 * m : 128 * (m + 1)]
                else:
                    part = h_scr[:, 128 * (m - len(LOCAL)) : 128 * (m - len(LOCAL) + 1)]
                if p != q:
                    part = pltpu.roll(part, (32 * (q - p)) % 128, 1)
                value = part if value is None else jnp.where(block == q, part, value)
            tiles.append(value if total is None else value + total[:, 128 * g : 128 * (g + 1)])
        edges = [pltpu.roll(tiles[-1], 32, 1)] + tiles + [pltpu.roll(tiles[0], 96, 1)]
        for g, part in enumerate(edges):
            high, low = split(part)
            x_scr[:N, 128 * g : 128 * (g + 1)] = high
            x_scr[N : 2 * N, 128 * g : 128 * (g + 1)] = low
            x_scr[2 * N :, 128 * g : 128 * (g + 1)] = high
        total = None
        for s in range(3):
            part = nn(b_ref[s], x_scr[:, 128 * (2 - s) : 128 * (2 - s + GRID)])
            total = part if total is None else total + part
    tiles = [total[:, 128 * g : 128 * (g + 1)] for g in range(GRID)]
    for m, entries in enumerate(RESULT):
        value = None
        for q, d in enumerate(entries):
            if d is None:
                continue
            g, p = place(d)
            part = tiles[g] if p == q else pltpu.roll(tiles[g], (32 * (q - p)) % 128, 1)
            value = part if value is None else jnp.where(block == q, part, value)
        result_ref[:, 128 * m : 128 * (m + 1)] = value
    for g in range(GRID):
        turned = tiles[g].T
        for q in range(4):
            d = GRID * q + g - BASE
            if 1 <= d <= 15:
                mirror_ref[15 - d] = turned[32 * q : 32 * (q + 1)]


def pack_kernel(result_ref, *outs):
    for k, out in enumerate(outs):
        for e in range(2):
            row = pl.multiple_of(target(k, e) * R, R)
            out[e] = result_ref[pl.ds(row, R), :]


def mirror_kernel(n_ref, mirror_ref, out_ref):
    out_ref[...] = n_ref[17:] + mirror_ref[...]


def join_kernel(n_ref, mirror_ref, *rest):
    received = rest[:4]
    other_ref, out_ref, r_scr = rest[4:]
    for k, ref in enumerate(received):
        r_scr[source(k, 0)] = ref[0]
        r_scr[source(k, 1)] = other_ref[k]
    for m, entries in enumerate(RESULT):
        for h in range(2):
            lanes = slice(128 * h, 128 * (h + 1))
            parts = [r_scr[4 * h + b, :, 128 * m : 128 * (m + 1)] for b in range(4)]
            for d, part in zip(entries, exchange_blocks(parts)):
                if d is not None:
                    out_ref[d, :, lanes] = n_ref[d, :, lanes] + part
    out_ref[17:] = mirror_ref[...]


PARAMS = pltpu.CompilerParams(vmem_limit_bytes=24 * 1024 * 1024)
SMEM = pl.BlockSpec(memory_space=pltpu.SMEM)
VMEM = pl.BlockSpec(memory_space=pltpu.VMEM)


def send(array, k, e):
    pairs = [(c, 2 * ((c // 2 + k) % 4) + (c + e) % 2) for c in range(8)]
    return lax.ppermute(array, "col", pairs)


def cost(units, elements):
    return pl.CostEstimate(flops=units * 18 * R * N * N, bytes_accessed=4 * elements, transcendentals=0)


def right_scratch(offsets):
    return [
        pltpu.VMEM((offsets * R, 3 * N), bf16),
        pltpu.VMEM((3, (offsets - 2) * R, N), f32),
    ]


def two_level(parts):
    parts = [parts[0]] + [send(parts[k], k, 0) for k in (1, 3, 2)]
    parts = [parts[0], parts[1], parts[3], parts[2]]
    return parts, send(jnp.stack([part[1] for part in parts]), 0, 1)


def body(noise_cov, couplings, shifts):
    *local, edge, first, taps_split = pl.pallas_call(
        local_kernel,
        out_shape=[jax.ShapeDtypeStruct((R, LOCAL_LANES), f32)] * 8
        + [jax.ShapeDtypeStruct((HALO, R, N), f32)] * 2
        + [jax.ShapeDtypeStruct((3, N, 3 * N), bf16)],
        in_specs=[SMEM, VMEM, VMEM],
        out_specs=[VMEM] * 11,
        scratch_shapes=right_scratch(23) + [pltpu.VMEM((8, R, LOCAL_LANES), f32)],
        compiler_params=PARAMS,
        cost_estimate=cost(57, 1 << 20),
        name="local_right_products",
    )(shifts, noise_cov, couplings)
    halo = lax.ppermute(noise_cov[R - HALO :], "off", [(o, (o + 1) % 16) for o in range(16)])
    local = [array if slot == (0, 0) else send(array, *slot) for array, slot in zip(local, SLOTS)]
    halos = pl.pallas_call(
        halo_kernel,
        out_shape=[jax.ShapeDtypeStruct((2, R, HALO_LANES), f32)] * 4,
        in_specs=[VMEM] * 3,
        out_specs=[VMEM] * 4,
        scratch_shapes=right_scratch(12) + [pltpu.VMEM((8, R, HALO_LANES), f32)],
        compiler_params=PARAMS,
        cost_estimate=cost(10, 1 << 19),
        name="halo_right_products",
    )(halo, first, taps_split)
    halos, other = two_level(halos)
    rows = pl.pallas_call(
        gather_kernel,
        out_shape=jax.ShapeDtypeStruct((N, LOCAL_LANES), f32),
        in_specs=[VMEM] * 8,
        out_specs=VMEM,
        compiler_params=PARAMS,
        cost_estimate=cost(300, 1 << 20),
        name="gather_rows",
    )(*local)
    result, mirror = pl.pallas_call(
        left_kernel,
        out_shape=[jax.ShapeDtypeStruct((N, OUT_LANES), f32), jax.ShapeDtypeStruct((15, R, N), f32)],
        in_specs=[VMEM] * 7,
        out_specs=[VMEM] * 2,
        scratch_shapes=[
            pltpu.VMEM((3 * N, 128 * (GRID + 2)), bf16),
            pltpu.VMEM((N, HALO_LANES), f32),
        ],
        compiler_params=PARAMS,
        cost_estimate=cost(72, 1 << 21),
        name="left_products",
    )(taps_split, rows, *halos, other)
    rows = pl.pallas_call(
        pack_kernel,
        out_shape=[jax.ShapeDtypeStruct((2, R, OUT_LANES), f32)] * 4,
        in_specs=[VMEM],
        out_specs=[VMEM] * 4,
        compiler_params=PARAMS,
        cost_estimate=cost(30, 1 << 19),
        name="pack",
    )(result)
    mirror = lax.ppermute(mirror, "off", [(o, 15 - o) for o in range(16)])
    mirror = pl.pallas_call(
        mirror_kernel,
        out_shape=jax.ShapeDtypeStruct((15, R, N), f32),
        in_specs=[VMEM] * 2,
        out_specs=VMEM,
        compiler_params=PARAMS,
        cost_estimate=cost(300, 1 << 19),
        name="join_mirror",
    )(noise_cov, mirror)
    rows, other = two_level(rows)
    return pl.pallas_call(
        join_kernel,
        out_shape=jax.ShapeDtypeStruct((R, R, N), f32),
        in_specs=[VMEM] * 7,
        out_specs=VMEM,
        scratch_shapes=[pltpu.VMEM((8, R, OUT_LANES), f32)],
        compiler_params=PARAMS,
        name="join",
    )(noise_cov, mirror, *rows, other)


def solution(mesh):
    return jax.shard_map(
        body,
        mesh=mesh,
        in_specs=(P("off", "col", None), P(), P()),
        out_specs=P("off", "col", None),
        check_vma=False,
    )
```

```python
import jax
import jax.numpy as jnp
from jax import lax
from jax.experimental import pallas as pl
from jax.experimental.pallas import tpu as pltpu
from jax.sharding import PartitionSpec as P

f32 = jnp.float32
bf16 = jnp.bfloat16

N = 256
R = 32
HALO = 6
GRID = 6
BASE = 3

def place(d):
    slot = d + BASE
    return slot % GRID, slot // GRID


def grid_tile(j, g, offsets):
    return [(j, GRID * q + g - BASE) if GRID * q + g - BASE in offsets else None for q in range(4)]


def local_tiles():
    tiles = [grid_tile(3, g, range(3, 20)) for g in range(GRID)]
    tiles += [grid_tile(2, g, range(2, 19)) for g in range(GRID)]
    tiles += [grid_tile(1, 5, range(1, 18))]
    free = [(tile, q) for tile in tiles[:-1] for q in range(4) if tile[q] is None]
    left = [d for d in range(1, 18) if place(d)[0] != 5]
    for tile, q in [f for f in free if f[1] == 3]:
        d = next(d for d in left if place(d)[1] == 3)
        left.remove(d)
        tile[q] = (1, d)
        free.remove((tile, q))
    for (tile, q), d in zip(free, left):
        tile[q] = (1, d)
    return tiles


LOCAL = local_tiles()
HALOS = [
    [(3, -3), (3, -2), (3, -1), (3, 0)],
    [(3, 1), (3, 2), (2, -2), (2, -1)],
    [(2, 0), (2, 1), (1, -1), (1, 0)],
]
WHERE = {entry: (m, p) for m, tile in enumerate(LOCAL + HALOS) for p, entry in enumerate(tile) if entry}
RESULT = [[5, 3, 9, 15], [11, 4, 10, 16], [0, 6, 12, 2], [1, 7, 13, 8]]
LAST = 14
OUT_ROWS = R * len(RESULT) + 8
LOCAL_LANES = 128 * len(LOCAL)
HALO_LANES = 128 * len(HALOS)
EARLY = [(2, 0), (2, 1)]
LATE = [(1, 0), (3, 0), (1, 1), (3, 1), (0, 1)]
SLOTS = EARLY + LATE + [(0, 0)]


def coordinates():
    col = lax.axis_index("col")
    return col // 2, col % 2


def target(k, e):
    z, core = coordinates()
    return 2 * ((z + k) % 4) + (core + e) % 2


def source(k, e):
    z, core = coordinates()
    return 2 * ((z + 4 - k) % 4) + (core + e) % 2


def split(x):
    high = x.astype(bf16)
    return high, (x - high.astype(f32)).astype(bf16)


def split_taps(c_ref, b_ref):
    for s in range(3):
        high, low = split(c_ref[s])
        k = 3 * N * s
        b_ref[:, k : k + N] = high
        b_ref[:, k + N : k + 2 * N] = high
        b_ref[:, k + 2 * N : k + 3 * N] = low


def block_of_lane(rows):
    return lax.broadcasted_iota(jnp.int32, (rows, 128), 1) // 32


def exchange_blocks(tiles):
    block = block_of_lane(tiles[0].shape[0])
    low = block < 2
    even = block % 2 == 0
    a = list(tiles)
    for q in (0, 1):
        x, y = a[q], a[q + 2]
        a[q] = jnp.where(low, x, pltpu.roll(y, 64, 1))
        a[q + 2] = jnp.where(low, pltpu.roll(x, 64, 1), y)
    for q in (0, 2):
        x, y = a[q], a[q + 1]
        a[q] = jnp.where(even, x, pltpu.roll(y, 32, 1))
        a[q + 1] = jnp.where(even, pltpu.roll(x, 96, 1), y)
    return a


def nt(x, y):
    return lax.dot_general(x, y, (((1,), (1,)), ((), ())), preferred_element_type=f32)


def nn(x, y):
    return lax.dot_general(x, y, (((1,), (0,)), ((), ())), preferred_element_type=f32)


def right_products(x, first, tiles, b_scr, x_scr, v_scr, m_ref):
    count = x.shape[0] // R
    start = {}
    for j in (1, 2, 3):
        high, low = split(x)
        x_scr[: count * R, :N] = high
        x_scr[: count * R, N : 2 * N] = low
        x_scr[: count * R, 2 * N :] = high
        count -= 2
        first += 1
        total = None
        for s in range(3):
            part = nt(x_scr[s * R : (s + count) * R], b_scr[:, 3 * N * s : 3 * N * (s + 1)])
            total = part if total is None else total + part
        x = total
        v_scr[j - 1, : count * R] = x
        start[j] = first
    for m, entries in enumerate(tiles):
        filler = next(entry for entry in entries if entry is not None)
        for h in range(2):
            parts = []
            for entry in entries:
                j, d = entry or filler
                row = (d - start[j]) * R
                parts.append(v_scr[j - 1, row : row + R, 128 * h : 128 * (h + 1)])
            for b, part in enumerate(exchange_blocks(parts)):
                m_ref[4 * h + b, :, 128 * m : 128 * (m + 1)] = part


def taps_kernel(shift_ref, n_ref, c_ref, edge_ref, own_ref, taps_ref):
    edge_ref[...] = n_ref[R - HALO :]
    own_ref[...] = n_ref[:23]
    for s in (-1, 0, 1):
        block = None
        for t in range(3):
            chosen = jnp.where(shift_ref[t] == s, f32(1), f32(0)) * c_ref[t]
            block = chosen if block is None else block + chosen
        taps_ref[s + 1] = block


def local_kernel(n_ref, c_ref, *rest):
    outs = rest[:8]
    first_ref, b_scr, x_scr, v_scr, m_scr = rest[8:]
    first_ref[...] = n_ref[:HALO]
    split_taps(c_ref, b_scr)
    right_products(n_ref[...].reshape(23 * R, N), 0, LOCAL, b_scr, x_scr, v_scr, m_scr)
    for out, slot in zip(outs, SLOTS):
        out[...] = m_scr[target(*slot)]


def halo_kernel(halo_ref, first_ref, c_ref, *rest):
    local = rest[:5]
    outs = rest[5:13]
    b_scr, x_scr, v_scr, m_scr = rest[13:]
    split_taps(c_ref, b_scr)
    x = jnp.concatenate([halo_ref[...].reshape(HALO * R, N), first_ref[...].reshape(HALO * R, N)], axis=0)
    right_products(x, -HALO, HALOS, b_scr, x_scr, v_scr, m_scr)
    for out, slot in zip(outs, SLOTS):
        lane = 0
        if slot in LATE:
            lane = LOCAL_LANES
            out[:, :lane] = local[LATE.index(slot)][...]
        out[:, lane:] = m_scr[target(*slot)]


def gather_kernel(*refs):
    r_ref = refs[11]
    local = dict(zip(EARLY + [(0, 0)], refs[:3]))
    for ref, slot in zip(refs[3:11], SLOTS):
        rows = pl.ds(pl.multiple_of(source(*slot) * R, R), R)
        if slot in local:
            r_ref[rows, :LOCAL_LANES] = local[slot][...]
            r_ref[rows, LOCAL_LANES:] = ref[...]
        else:
            r_ref[rows, :] = ref[...]


def left_kernel(c_ref, r_ref, result_ref, mirror_ref, b_scr, x_scr):
    split_taps(c_ref, b_scr)
    block = block_of_lane(N)
    total = None
    for j in (3, 2, 1):
        tiles = []
        for g in range(GRID):
            value = None
            for q in range(4):
                entry = (j, GRID * q + g - BASE)
                if entry not in WHERE:
                    continue
                m, p = WHERE[entry]
                part = r_ref[:, 128 * m : 128 * (m + 1)]
                if p != q:
                    part = pltpu.roll(part, (32 * (q - p)) % 128, 1)
                value = part if value is None else jnp.where(block == q, part, value)
            tiles.append(value if total is None else value + total[:, 128 * g : 128 * (g + 1)])
        edges = [pltpu.roll(tiles[-1], 32, 1)] + tiles + [pltpu.roll(tiles[0], 96, 1)]
        for g, part in enumerate(edges):
            high, low = split(part)
            for s in range(3):
                t = g - 2 + s
                if 0 <= t < GRID:
                    k = 3 * N * s
                    lanes = slice(128 * t, 128 * (t + 1))
                    x_scr[k : k + N, lanes] = high
                    x_scr[k + N : k + 2 * N, lanes] = low
                    x_scr[k + 2 * N : k + 3 * N, lanes] = high
        total = nn(b_scr[...], x_scr[...])
    tiles = [total[:, 128 * g : 128 * (g + 1)] for g in range(GRID)]
    for m, entries in enumerate(RESULT):
        value = None
        for q, d in enumerate(entries):
            if d is None:
                continue
            g, p = place(d)
            part = tiles[g] if p == q else pltpu.roll(tiles[g], (32 * (q - p)) % 128, 1)
            value = part if value is None else jnp.where(block == q, part, value)
        result_ref[:, R * m : R * (m + 1), :] = value.reshape(8, R, 128)
    g, p = place(LAST)
    quarters = tiles[g].reshape(8, 4, 8, 128)
    block = block_of_lane(64)
    value = None
    for a in range(4):
        part = quarters[:, a].reshape(64, 128)
        part = part if a == p else pltpu.roll(part, (32 * (a - p)) % 128, 1)
        value = part if value is None else jnp.where(block == a, part, value)
    result_ref[:, OUT_ROWS - 8 :, :] = value.reshape(8, 8, 128)
    for g in range(GRID):
        turned = tiles[g].T
        for q in range(4):
            d = GRID * q + g - BASE
            if 1 <= d <= 15:
                mirror_ref[15 - d] = turned[32 * q : 32 * (q + 1)]


def pack_kernel(result_ref, *outs):
    for k, out in enumerate(outs):
        for e in range(2):
            out[e] = result_ref[target(k, e)]


def mirror_kernel(n_ref, mirror_ref, out_ref):
    out_ref[...] = n_ref[17:] + mirror_ref[...]


def join_kernel(n_ref, mirror_ref, *rest):
    received = rest[:4]
    other_ref, out_ref, r_scr, o_scr, sems = rest[4:]
    copies = [pltpu.make_async_copy(mirror_ref, out_ref.at[pl.ds(17, 15)], sems.at[17])]
    copies[0].start()
    for k, ref in enumerate(received):
        r_scr[source(k, 0)] = ref[0]
        r_scr[source(k, 1)] = other_ref[k]
    halves = (slice(0, 128), slice(128, 256))

    def send_out(d):
        copies.append(pltpu.make_async_copy(o_scr.at[d], out_ref.at[d], sems.at[d]))
        copies[-1].start()

    for m, entries in enumerate(RESULT):
        for h, lanes in enumerate(halves):
            parts = [r_scr[4 * h + b, R * m : R * (m + 1)] for b in range(4)]
            for d, part in zip(entries, exchange_blocks(parts)):
                o_scr[d, :, lanes] = n_ref[d, :, lanes] + part
        for d in entries:
            send_out(d)
    for h, lanes in enumerate(halves):
        parts = [r_scr[4 * h + b, OUT_ROWS - 8 :] for b in range(4)]
        for a, part in enumerate(exchange_blocks(parts)):
            rows = slice(8 * a, 8 * (a + 1))
            o_scr[LAST, rows, lanes] = n_ref[LAST, rows, lanes] + part
    send_out(LAST)
    for copy in copies:
        copy.wait()


PARAMS = pltpu.CompilerParams(vmem_limit_bytes=24 * 1024 * 1024)
HBM = pl.BlockSpec(memory_space=pl.ANY)
SMEM = pl.BlockSpec(memory_space=pltpu.SMEM)
VMEM = pl.BlockSpec(memory_space=pltpu.VMEM)


def send(array, k, e):
    pairs = [(c, 2 * ((c // 2 + k) % 4) + (c + e) % 2) for c in range(8)]
    return lax.ppermute(array, "col", pairs)


def cost(units, elements):
    return pl.CostEstimate(flops=units * 18 * R * N * N, bytes_accessed=4 * elements, transcendentals=0)


def right_scratch(offsets):
    return [
        pltpu.VMEM((N, 9 * N), bf16),
        pltpu.VMEM((offsets * R, 3 * N), bf16),
        pltpu.VMEM((3, (offsets - 2) * R, N), f32),
    ]


def two_level(parts):
    parts = [parts[0]] + [send(parts[k], k, 0) for k in (1, 3, 2)]
    parts = [parts[0], parts[1], parts[3], parts[2]]
    return parts, send(jnp.stack([part[1] for part in parts]), 0, 1)


def body(noise_cov, couplings, shifts):
    edge, own, taps = pl.pallas_call(
        taps_kernel,
        out_shape=[
            jax.ShapeDtypeStruct((HALO, R, N), f32),
            jax.ShapeDtypeStruct((23, R, N), f32),
            jax.ShapeDtypeStruct((3, N, N), f32),
        ],
        in_specs=[SMEM, VMEM, VMEM],
        out_specs=[VMEM] * 3,
        compiler_params=PARAMS,
        name="taps",
    )(shifts, noise_cov, couplings)
    halo = lax.ppermute(edge, "off", [(o, (o + 1) % 16) for o in range(16)])
    *local, first = pl.pallas_call(
        local_kernel,
        out_shape=[jax.ShapeDtypeStruct((R, LOCAL_LANES), f32)] * 8 + [jax.ShapeDtypeStruct((HALO, R, N), f32)],
        in_specs=[VMEM, VMEM],
        out_specs=[VMEM] * 9,
        scratch_shapes=right_scratch(23) + [pltpu.VMEM((8, R, LOCAL_LANES), f32)],
        compiler_params=PARAMS,
        cost_estimate=cost(57, 1 << 20),
        name="local_right_products",
    )(own, taps)
    local = dict(zip(SLOTS, local))
    early = [send(local[slot], *slot) for slot in EARLY]
    halos = pl.pallas_call(
        halo_kernel,
        out_shape=[
            jax.ShapeDtypeStruct((R, HALO_LANES + LOCAL_LANES * (slot in LATE)), f32) for slot in SLOTS
        ],
        in_specs=[VMEM] * 8,
        out_specs=[VMEM] * 8,
        scratch_shapes=right_scratch(12) + [pltpu.VMEM((8, R, HALO_LANES), f32)],
        compiler_params=PARAMS,
        cost_estimate=cost(10, 1 << 19),
        name="halo_right_products",
    )(halo, first, taps, *[local[slot] for slot in LATE])
    halos = [array if slot == (0, 0) else send(array, *slot) for array, slot in zip(halos, SLOTS)]
    rows = pl.pallas_call(
        gather_kernel,
        out_shape=jax.ShapeDtypeStruct((N, LOCAL_LANES + HALO_LANES), f32),
        in_specs=[VMEM] * 11,
        out_specs=VMEM,
        compiler_params=PARAMS,
        cost_estimate=cost(10, 1 << 20),
        name="gather_rows",
    )(*early, local[0, 0], *halos)
    result, mirror = pl.pallas_call(
        left_kernel,
        out_shape=[jax.ShapeDtypeStruct((8, OUT_ROWS, 128), f32), jax.ShapeDtypeStruct((15, R, N), f32)],
        in_specs=[VMEM] * 2,
        out_specs=[VMEM] * 2,
        scratch_shapes=[
            pltpu.VMEM((N, 9 * N), bf16),
            pltpu.VMEM((9 * N, 128 * GRID), bf16),
        ],
        compiler_params=PARAMS,
        cost_estimate=cost(72, 1 << 21),
        name="left_products",
    )(taps, rows)
    rows = pl.pallas_call(
        pack_kernel,
        out_shape=[jax.ShapeDtypeStruct((2, OUT_ROWS, 128), f32)] * 4,
        in_specs=[VMEM],
        out_specs=[VMEM] * 4,
        compiler_params=PARAMS,
        cost_estimate=cost(30, 1 << 19),
        name="pack",
    )(result)
    mirror = lax.ppermute(mirror, "off", [(o, 15 - o) for o in range(16)])
    mirror = pl.pallas_call(
        mirror_kernel,
        out_shape=jax.ShapeDtypeStruct((15, R, N), f32),
        in_specs=[VMEM] * 2,
        out_specs=VMEM,
        compiler_params=PARAMS,
        cost_estimate=cost(300, 1 << 19),
        name="join_mirror",
    )(noise_cov, mirror)
    rows, other = two_level(rows)
    return pl.pallas_call(
        join_kernel,
        out_shape=jax.ShapeDtypeStruct((R, R, N), f32),
        in_specs=[VMEM] * 7,
        out_specs=HBM,
        scratch_shapes=[
            pltpu.VMEM((8, OUT_ROWS, 128), f32),
            pltpu.VMEM((17, R, N), f32),
            pltpu.SemaphoreType.DMA((18,)),
        ],
        compiler_params=PARAMS,
        name="join",
    )(noise_cov, mirror, *rows, other)


def solution(mesh):
    return jax.shard_map(
        body,
        mesh=mesh,
        in_specs=(P("off", "col", None), P(), P()),
        out_specs=P("off", "col", None),
        check_vma=False,
    )
```

```python
import jax
import jax.numpy as jnp
from jax import lax
from jax.experimental import pallas as pl
from jax.experimental.pallas import tpu as pltpu
from jax.sharding import PartitionSpec as P

f32 = jnp.float32
bf16 = jnp.bfloat16

N = 256
R = 32
HALO = 6
GRID = 6
BASE = 3

def place(d):
    slot = d + BASE
    return slot % GRID, slot // GRID


def grid_tile(j, g, offsets):
    return [(j, GRID * q + g - BASE) if GRID * q + g - BASE in offsets else None for q in range(4)]


def local_tiles():
    tiles = [grid_tile(3, g, range(3, 20)) for g in range(GRID)]
    tiles += [grid_tile(2, g, range(2, 19)) for g in range(GRID)]
    tiles += [grid_tile(1, 5, range(1, 18))]
    free = [(tile, q) for tile in tiles[:-1] for q in range(4) if tile[q] is None]
    left = [d for d in range(1, 18) if place(d)[0] != 5]
    for tile, q in [f for f in free if f[1] == 3]:
        d = next(d for d in left if place(d)[1] == 3)
        left.remove(d)
        tile[q] = (1, d)
        free.remove((tile, q))
    for (tile, q), d in zip(free, left):
        tile[q] = (1, d)
    return tiles


LOCAL = local_tiles()
HALOS = [
    [(3, -3), (3, -2), (3, -1), (3, 0)],
    [(3, 1), (3, 2), (2, -2), (2, -1)],
    [(2, 0), (2, 1), (1, -1), (1, 0)],
]
WHERE = {entry: (m, p) for m, tile in enumerate(LOCAL + HALOS) for p, entry in enumerate(tile) if entry}
RESULT = [[5, 3, 9, 15], [11, 4, 10, 16], [0, 6, 12, 2], [1, 7, 13, 8]]
LAST = 14
DISTANCES = (0, 2, 1, 3)
OUT_ROWS = R * len(RESULT) + 8
LOCAL_LANES = 128 * len(LOCAL)
HALO_LANES = 128 * len(HALOS)
EARLY = [(2, 0), (2, 1)]
LATE = [(1, 0), (3, 0), (1, 1), (3, 1), (0, 1)]
SLOTS = EARLY + LATE + [(0, 0)]
SECOND = [(1, 0), (3, 0), (2, 0), (2, 1), (1, 1), (3, 1), (0, 1), (0, 0)]


def coordinates():
    col = lax.axis_index("col")
    return col // 2, col % 2


def target(k, e):
    z, core = coordinates()
    return 2 * ((z + k) % 4) + (core + e) % 2


def source(k, e):
    z, core = coordinates()
    return 2 * ((z + 4 - k) % 4) + (core + e) % 2


def split(x):
    high = x.astype(bf16)
    return high, (x - high.astype(f32)).astype(bf16)


def split_taps(c_ref, b_ref):
    for s in range(3):
        high, low = split(c_ref[s])
        k = 3 * N * s
        b_ref[:, k : k + N] = high
        b_ref[:, k + N : k + 2 * N] = high
        b_ref[:, k + 2 * N : k + 3 * N] = low


def block_of_lane(rows):
    return lax.broadcasted_iota(jnp.int32, (rows, 128), 1) // 32


def exchange_blocks(tiles):
    block = block_of_lane(tiles[0].shape[0])
    low = block < 2
    even = block % 2 == 0
    a = list(tiles)
    for q in (0, 1):
        x, y = a[q], a[q + 2]
        a[q] = jnp.where(low, x, pltpu.roll(y, 64, 1))
        a[q + 2] = jnp.where(low, pltpu.roll(x, 64, 1), y)
    for q in (0, 2):
        x, y = a[q], a[q + 1]
        a[q] = jnp.where(even, x, pltpu.roll(y, 32, 1))
        a[q + 1] = jnp.where(even, pltpu.roll(x, 96, 1), y)
    return a


def nt(x, y):
    return lax.dot_general(x, y, (((1,), (1,)), ((), ())), preferred_element_type=f32)


def nn(x, y):
    return lax.dot_general(x, y, (((1,), (0,)), ((), ())), preferred_element_type=f32)


def right_products(x, first, tiles, b_scr, x_scr, v_scr, m_ref):
    count = x.shape[0] // R
    start = {}
    for j in (1, 2, 3):
        high, low = split(x)
        x_scr[: count * R, :N] = high
        x_scr[: count * R, N : 2 * N] = low
        x_scr[: count * R, 2 * N :] = high
        count -= 2
        first += 1
        total = None
        for s in range(3):
            part = nt(x_scr[s * R : (s + count) * R], b_scr[:, 3 * N * s : 3 * N * (s + 1)])
            total = part if total is None else total + part
        x = total
        v_scr[j - 1, : count * R] = x
        start[j] = first
    for m, entries in enumerate(tiles):
        filler = next(entry for entry in entries if entry is not None)
        for h in range(2):
            parts = []
            for entry in entries:
                j, d = entry or filler
                row = (d - start[j]) * R
                parts.append(v_scr[j - 1, row : row + R, 128 * h : 128 * (h + 1)])
            for b, part in enumerate(exchange_blocks(parts)):
                m_ref[4 * h + b, :, 128 * m : 128 * (m + 1)] = part


def edge_kernel(n_ref, edge_ref, own_ref):
    edge_ref[...] = n_ref[R - HALO :]
    own_ref[...] = n_ref[:23]


def local_kernel(shift_ref, n_ref, c_ref, *rest):
    outs = rest[:8]
    first_ref, taps_ref, b_scr, x_scr, v_scr, m_scr = rest[8:]
    first_ref[...] = n_ref[:HALO]
    for s in (-1, 0, 1):
        block = None
        for t in range(3):
            chosen = jnp.where(shift_ref[t] == s, f32(1), f32(0)) * c_ref[t]
            block = chosen if block is None else block + chosen
        taps_ref[s + 1] = block
    split_taps(taps_ref, b_scr)
    right_products(n_ref[...].reshape(23 * R, N), 0, LOCAL, b_scr, x_scr, v_scr, m_scr)
    for out, slot in zip(outs, SLOTS):
        out[...] = m_scr[target(*slot)]


def halo_kernel(halo_ref, first_ref, c_ref, *rest):
    local = rest[:5]
    outs = rest[5:13]
    b_scr, x_scr, v_scr, m_scr = rest[13:]
    split_taps(c_ref, b_scr)
    x = jnp.concatenate([halo_ref[...].reshape(HALO * R, N), first_ref[...].reshape(HALO * R, N)], axis=0)
    right_products(x, -HALO, HALOS, b_scr, x_scr, v_scr, m_scr)
    for out, slot in zip(outs, SECOND):
        lane = 0
        if slot in LATE:
            lane = LOCAL_LANES
            out[:, :lane] = local[LATE.index(slot)][...]
        out[:, lane:] = m_scr[target(*slot)]


def gather_kernel(*refs):
    r_ref = refs[11]
    local = dict(zip(EARLY + [(0, 0)], refs[:3]))
    for ref, slot in zip(refs[3:11], SECOND):
        rows = pl.ds(pl.multiple_of(source(*slot) * R, R), R)
        if slot in local:
            r_ref[rows, :LOCAL_LANES] = local[slot][...]
            r_ref[rows, LOCAL_LANES:] = ref[...]
        else:
            r_ref[rows, :] = ref[...]


def left_kernel(c_ref, r_ref, result_ref, mirror_ref, b_scr, x_scr):
    split_taps(c_ref, b_scr)
    block = block_of_lane(N)
    total = None
    for j in (3, 2, 1):
        tiles = []
        for g in range(GRID):
            value = None
            for q in range(4):
                entry = (j, GRID * q + g - BASE)
                if entry not in WHERE:
                    continue
                m, p = WHERE[entry]
                part = r_ref[:, 128 * m : 128 * (m + 1)]
                if p != q:
                    part = pltpu.roll(part, (32 * (q - p)) % 128, 1)
                value = part if value is None else jnp.where(block == q, part, value)
            tiles.append(value if total is None else value + total[:, 128 * g : 128 * (g + 1)])
        edges = [pltpu.roll(tiles[-1], 32, 1)] + tiles + [pltpu.roll(tiles[0], 96, 1)]
        for g, part in enumerate(edges):
            high, low = split(part)
            for s in range(3):
                t = g - 2 + s
                if 0 <= t < GRID:
                    k = 3 * N * s
                    lanes = slice(128 * t, 128 * (t + 1))
                    x_scr[k : k + N, lanes] = high
                    x_scr[k + N : k + 2 * N, lanes] = low
                    x_scr[k + 2 * N : k + 3 * N, lanes] = high
        total = nn(b_scr[...], x_scr[...])
    tiles = [total[:, 128 * g : 128 * (g + 1)] for g in range(GRID)]
    for m, entries in enumerate(RESULT):
        value = None
        for q, d in enumerate(entries):
            if d is None:
                continue
            g, p = place(d)
            part = tiles[g] if p == q else pltpu.roll(tiles[g], (32 * (q - p)) % 128, 1)
            value = part if value is None else jnp.where(block == q, part, value)
        result_ref[:, R * m : R * (m + 1), :] = value.reshape(8, R, 128)
    g, p = place(LAST)
    quarters = tiles[g].reshape(8, 4, 8, 128)
    block = block_of_lane(64)
    value = None
    for a in range(4):
        part = quarters[:, a].reshape(64, 128)
        part = part if a == p else pltpu.roll(part, (32 * (a - p)) % 128, 1)
        value = part if value is None else jnp.where(block == a, part, value)
    result_ref[:, OUT_ROWS - 8 :, :] = value.reshape(8, 8, 128)
    for g in range(GRID):
        turned = tiles[g].T
        for q in range(4):
            d = GRID * q + g - BASE
            if 1 <= d <= 15:
                mirror_ref[15 - d] = turned[32 * q : 32 * (q + 1)]


def pack_kernel(result_ref, *outs):
    for k, out in zip(DISTANCES, outs):
        for e in range(2):
            out[e] = result_ref[target(k, e)]


def mirror_kernel(n_ref, mirror_ref, out_ref):
    out_ref[...] = n_ref[17:] + mirror_ref[...]


def join_kernel(n_ref, mirror_ref, *rest):
    received = rest[:4]
    other_ref, out_ref, r_scr, o_scr, sems = rest[4:]
    copies = [pltpu.make_async_copy(mirror_ref, out_ref.at[pl.ds(17, 15)], sems.at[17])]
    copies[0].start()
    for n, (k, ref) in enumerate(zip(DISTANCES, received)):
        r_scr[source(k, 0)] = ref[0]
        r_scr[source(k, 1)] = other_ref[n]
    halves = (slice(0, 128), slice(128, 256))

    def send_out(d):
        copies.append(pltpu.make_async_copy(o_scr.at[d], out_ref.at[d], sems.at[d]))
        copies[-1].start()

    for m, entries in enumerate(RESULT):
        for h, lanes in enumerate(halves):
            parts = [r_scr[4 * h + b, R * m : R * (m + 1)] for b in range(4)]
            for d, part in zip(entries, exchange_blocks(parts)):
                o_scr[d, :, lanes] = n_ref[d, :, lanes] + part
        for d in entries:
            send_out(d)
    for h, lanes in enumerate(halves):
        parts = [r_scr[4 * h + b, OUT_ROWS - 8 :] for b in range(4)]
        for a, part in enumerate(exchange_blocks(parts)):
            rows = slice(8 * a, 8 * (a + 1))
            o_scr[LAST, rows, lanes] = n_ref[LAST, rows, lanes] + part
    send_out(LAST)
    for copy in copies:
        copy.wait()


PARAMS = pltpu.CompilerParams(vmem_limit_bytes=24 * 1024 * 1024)
HBM = pl.BlockSpec(memory_space=pl.ANY)
SMEM = pl.BlockSpec(memory_space=pltpu.SMEM)
VMEM = pl.BlockSpec(memory_space=pltpu.VMEM)


def send(array, k, e):
    pairs = [(c, 2 * ((c // 2 + k) % 4) + (c + e) % 2) for c in range(8)]
    return lax.ppermute(array, "col", pairs)


def cost(units, elements):
    return pl.CostEstimate(flops=units * 18 * R * N * N, bytes_accessed=4 * elements, transcendentals=0)


def right_scratch(offsets):
    return [
        pltpu.VMEM((N, 9 * N), bf16),
        pltpu.VMEM((offsets * R, 3 * N), bf16),
        pltpu.VMEM((3, (offsets - 2) * R, N), f32),
    ]


def two_level(parts):
    parts = [part if k == 0 else send(part, k, 0) for k, part in zip(DISTANCES, parts)]
    return parts, send(jnp.stack([part[1] for part in parts]), 0, 1)


def body(noise_cov, couplings, shifts):
    edge, own = pl.pallas_call(
        edge_kernel,
        out_shape=[jax.ShapeDtypeStruct((HALO, R, N), f32), jax.ShapeDtypeStruct((23, R, N), f32)],
        in_specs=[VMEM],
        out_specs=[VMEM] * 2,
        compiler_params=PARAMS,
        cost_estimate=cost(200, 1 << 20),
        name="edge",
    )(noise_cov)
    halo = lax.ppermute(edge, "off", [(o, (o + 1) % 16) for o in range(16)])
    *local, first, taps = pl.pallas_call(
        local_kernel,
        out_shape=[jax.ShapeDtypeStruct((R, LOCAL_LANES), f32)] * 8 + [jax.ShapeDtypeStruct((HALO, R, N), f32), jax.ShapeDtypeStruct((3, N, N), f32)],
        in_specs=[SMEM, VMEM, VMEM],
        out_specs=[VMEM] * 10,
        scratch_shapes=right_scratch(23) + [pltpu.VMEM((8, R, LOCAL_LANES), f32)],
        compiler_params=PARAMS,
        cost_estimate=cost(57, 1 << 20),
        name="local_right_products",
    )(shifts, own, couplings)
    local = dict(zip(SLOTS, local))
    early = [send(local[slot], *slot) for slot in EARLY]
    halos = pl.pallas_call(
        halo_kernel,
        out_shape=[
            jax.ShapeDtypeStruct((R, HALO_LANES + LOCAL_LANES * (slot in LATE)), f32) for slot in SECOND
        ],
        in_specs=[VMEM] * 8,
        out_specs=[VMEM] * 8,
        scratch_shapes=right_scratch(12) + [pltpu.VMEM((8, R, HALO_LANES), f32)],
        compiler_params=PARAMS,
        cost_estimate=cost(10, 1 << 19),
        name="halo_right_products",
    )(halo, first, taps, *[local[slot] for slot in LATE])
    halos = [array if slot == (0, 0) else send(array, *slot) for array, slot in zip(halos, SECOND)]
    rows = pl.pallas_call(
        gather_kernel,
        out_shape=jax.ShapeDtypeStruct((N, LOCAL_LANES + HALO_LANES), f32),
        in_specs=[VMEM] * 11,
        out_specs=VMEM,
        compiler_params=PARAMS,
        cost_estimate=cost(10, 1 << 20),
        name="gather_rows",
    )(*early, local[0, 0], *halos)
    result, mirror = pl.pallas_call(
        left_kernel,
        out_shape=[jax.ShapeDtypeStruct((8, OUT_ROWS, 128), f32), jax.ShapeDtypeStruct((15, R, N), f32)],
        in_specs=[VMEM] * 2,
        out_specs=[VMEM] * 2,
        scratch_shapes=[
            pltpu.VMEM((N, 9 * N), bf16),
            pltpu.VMEM((9 * N, 128 * GRID), bf16),
        ],
        compiler_params=PARAMS,
        cost_estimate=cost(72, 1 << 21),
        name="left_products",
    )(taps, rows)
    rows = pl.pallas_call(
        pack_kernel,
        out_shape=[jax.ShapeDtypeStruct((2, OUT_ROWS, 128), f32)] * 4,
        in_specs=[VMEM],
        out_specs=[VMEM] * 4,
        compiler_params=PARAMS,
        cost_estimate=cost(30, 1 << 19),
        name="pack",
    )(result)
    mirror = lax.ppermute(mirror, "off", [(o, 15 - o) for o in range(16)])
    mirror = pl.pallas_call(
        mirror_kernel,
        out_shape=jax.ShapeDtypeStruct((15, R, N), f32),
        in_specs=[VMEM] * 2,
        out_specs=VMEM,
        compiler_params=PARAMS,
        cost_estimate=cost(300, 1 << 19),
        name="join_mirror",
    )(noise_cov, mirror)
    rows, other = two_level(rows)
    return pl.pallas_call(
        join_kernel,
        out_shape=jax.ShapeDtypeStruct((R, R, N), f32),
        in_specs=[VMEM] * 7,
        out_specs=HBM,
        scratch_shapes=[
            pltpu.VMEM((8, OUT_ROWS, 128), f32),
            pltpu.VMEM((17, R, N), f32),
            pltpu.SemaphoreType.DMA((18,)),
        ],
        compiler_params=PARAMS,
        name="join",
    )(noise_cov, mirror, *rows, other)


def solution(mesh):
    return jax.shard_map(
        body,
        mesh=mesh,
        in_specs=(P("off", "col", None), P(), P()),
        out_specs=P("off", "col", None),
        check_vma=False,
    )
```

```python
import jax
import jax.numpy as jnp
from jax import lax
from jax.experimental import pallas as pl
from jax.experimental.pallas import tpu as pltpu
from jax.sharding import PartitionSpec as P

f32 = jnp.float32
bf16 = jnp.bfloat16

N = 256
R = 32
HALO = 6
GRID = 6
BASE = 3

def place(d):
    slot = d + BASE
    return slot % GRID, slot // GRID


def grid_tile(j, g, offsets):
    return [(j, GRID * q + g - BASE) if GRID * q + g - BASE in offsets else None for q in range(4)]


def local_tiles():
    tiles = [grid_tile(3, g, range(3, 20)) for g in range(GRID)]
    tiles += [grid_tile(2, g, range(2, 19)) for g in range(GRID)]
    tiles += [grid_tile(1, 5, range(1, 18))]
    free = [(tile, q) for tile in tiles[:-1] for q in range(4) if tile[q] is None]
    left = [d for d in range(1, 18) if place(d)[0] != 5]
    for tile, q in [f for f in free if f[1] == 3]:
        d = next(d for d in left if place(d)[1] == 3)
        left.remove(d)
        tile[q] = (1, d)
        free.remove((tile, q))
    for (tile, q), d in zip(free, left):
        tile[q] = (1, d)
    return tiles


LOCAL = local_tiles()
HALOS = [
    [(3, -3), (3, -2), (3, -1), (3, 0)],
    [(3, 1), (3, 2), (2, -2), (2, -1)],
    [(2, 0), (2, 1), (1, -1), (1, 0)],
]
WHERE = {entry: (m, p) for m, tile in enumerate(LOCAL + HALOS) for p, entry in enumerate(tile) if entry}
RESULT = [[5, 3, 9, 15], [11, 4, 10, 16], [0, 6, 12, 2], [1, 7, 13, 8]]
LAST = 14
DISTANCES = (0, 2, 1, 3)
OUT_ROWS = R * len(RESULT) + 8
LOCAL_LANES = 128 * len(LOCAL)
HALO_LANES = 128 * len(HALOS)
EARLY = [(2, 0), (2, 1)]
LATE = [(1, 0), (3, 0), (1, 1), (3, 1), (0, 1)]
SLOTS = EARLY + LATE + [(0, 0)]
SECOND = [(1, 0), (3, 0), (2, 0), (2, 1), (1, 1), (3, 1), (0, 1), (0, 0)]


def coordinates():
    col = lax.axis_index("col")
    return col // 2, col % 2


def target(k, e):
    z, core = coordinates()
    return 2 * ((z + k) % 4) + (core + e) % 2


def source(k, e):
    z, core = coordinates()
    return 2 * ((z + 4 - k) % 4) + (core + e) % 2


def split(x):
    high = x.astype(bf16)
    return high, (x - high.astype(f32)).astype(bf16)


def split_taps(c_ref, b_ref):
    for s in range(3):
        high, low = split(c_ref[s])
        k = 3 * N * s
        b_ref[:, k : k + N] = high
        b_ref[:, k + N : k + 2 * N] = high
        b_ref[:, k + 2 * N : k + 3 * N] = low


def block_of_lane(rows):
    return lax.broadcasted_iota(jnp.int32, (rows, 128), 1) // 32


def exchange_blocks(tiles):
    block = block_of_lane(tiles[0].shape[0])
    low = block < 2
    even = block % 2 == 0
    a = list(tiles)
    for q in (0, 1):
        x, y = a[q], a[q + 2]
        a[q] = jnp.where(low, x, pltpu.roll(y, 64, 1))
        a[q + 2] = jnp.where(low, pltpu.roll(x, 64, 1), y)
    for q in (0, 2):
        x, y = a[q], a[q + 1]
        a[q] = jnp.where(even, x, pltpu.roll(y, 32, 1))
        a[q + 1] = jnp.where(even, pltpu.roll(x, 96, 1), y)
    return a


def nt(x, y):
    return lax.dot_general(x, y, (((1,), (1,)), ((), ())), preferred_element_type=f32)


def nn(x, y):
    return lax.dot_general(x, y, (((1,), (0,)), ((), ())), preferred_element_type=f32)


def right_products(x, first, tiles, b_scr, x_scr, v_scr, m_ref):
    count = x.shape[0] // R
    start = {}
    for j in (1, 2, 3):
        high, low = split(x)
        x_scr[: count * R, :N] = high
        x_scr[: count * R, N : 2 * N] = low
        x_scr[: count * R, 2 * N :] = high
        count -= 2
        first += 1
        total = None
        for s in range(3):
            part = nt(x_scr[s * R : (s + count) * R], b_scr[:, 3 * N * s : 3 * N * (s + 1)])
            total = part if total is None else total + part
        x = total
        v_scr[j - 1, : count * R] = x
        start[j] = first
    for m, entries in enumerate(tiles):
        filler = next(entry for entry in entries if entry is not None)
        for h in range(2):
            parts = []
            for entry in entries:
                j, d = entry or filler
                row = (d - start[j]) * R
                parts.append(v_scr[j - 1, row : row + R, 128 * h : 128 * (h + 1)])
            for b, part in enumerate(exchange_blocks(parts)):
                m_ref[4 * h + b, :, 128 * m : 128 * (m + 1)] = part


def edge_kernel(n_ref, edge_ref, own_ref):
    edge_ref[...] = n_ref[R - HALO :]
    own_ref[...] = n_ref[:23]


def local_kernel(shift_ref, n_ref, c_ref, *rest):
    outs = rest[:8]
    first_ref, taps_ref, b_scr, x_scr, v_scr, m_scr = rest[8:]
    first_ref[...] = n_ref[:HALO]
    for s in (-1, 0, 1):
        block = None
        for t in range(3):
            chosen = jnp.where(shift_ref[t] == s, f32(1), f32(0)) * c_ref[t]
            block = chosen if block is None else block + chosen
        taps_ref[s + 1] = block
    split_taps(taps_ref, b_scr)
    right_products(n_ref[...].reshape(23 * R, N), 0, LOCAL, b_scr, x_scr, v_scr, m_scr)
    for out, slot in zip(outs, SLOTS):
        out[...] = m_scr[target(*slot)]


def halo_kernel(halo_ref, first_ref, c_ref, *rest):
    local = rest[:5]
    outs = rest[5:13]
    b_scr, x_scr, v_scr, m_scr = rest[13:]
    split_taps(c_ref, b_scr)
    x = jnp.concatenate([halo_ref[...].reshape(HALO * R, N), first_ref[...].reshape(HALO * R, N)], axis=0)
    right_products(x, -HALO, HALOS, b_scr, x_scr, v_scr, m_scr)
    for out, slot in zip(outs, SECOND):
        lane = 0
        if slot in LATE:
            lane = LOCAL_LANES
            out[:, :lane] = local[LATE.index(slot)][...]
        out[:, lane:] = m_scr[target(*slot)]


def gather_kernel(*refs):
    r_ref = refs[11]
    local = dict(zip(EARLY + [(0, 0)], refs[:3]))
    for ref, slot in zip(refs[3:11], SECOND):
        rows = pl.ds(pl.multiple_of(source(*slot) * R, R), R)
        if slot in local:
            r_ref[rows, :LOCAL_LANES] = local[slot][...]
            r_ref[rows, LOCAL_LANES:] = ref[...]
        else:
            r_ref[rows, :] = ref[...]


def left_kernel(c_ref, r_ref, tiles_ref, mirror_ref, b_scr, x_scr):
    split_taps(c_ref, b_scr)
    block = block_of_lane(N)
    total = None
    for j in (3, 2, 1):
        tiles = []
        for g in range(GRID):
            value = None
            for q in range(4):
                entry = (j, GRID * q + g - BASE)
                if entry not in WHERE:
                    continue
                m, p = WHERE[entry]
                part = r_ref[:, 128 * m : 128 * (m + 1)]
                if p != q:
                    part = pltpu.roll(part, (32 * (q - p)) % 128, 1)
                value = part if value is None else jnp.where(block == q, part, value)
            tiles.append(value if total is None else value + total[:, 128 * g : 128 * (g + 1)])
        edges = [pltpu.roll(tiles[-1], 32, 1)] + tiles + [pltpu.roll(tiles[0], 96, 1)]
        for g, part in enumerate(edges):
            high, low = split(part)
            for s in range(3):
                t = g - 2 + s
                if 0 <= t < GRID:
                    k = 3 * N * s
                    lanes = slice(128 * t, 128 * (t + 1))
                    x_scr[k : k + N, lanes] = high
                    x_scr[k + N : k + 2 * N, lanes] = low
                    x_scr[k + 2 * N : k + 3 * N, lanes] = high
        total = nn(b_scr[...], x_scr[...])
    tiles = [total[:, 128 * g : 128 * (g + 1)] for g in range(GRID)]
    for g in range(GRID):
        turned = tiles[g].T
        for q in range(4):
            d = GRID * q + g - BASE
            if 1 <= d <= 15:
                mirror_ref[15 - d] = turned[32 * q : 32 * (q + 1)]
    tiles_ref[...] = total


def pack_kernel(tiles_ref, *rest):
    outs = rest[:4]
    result_ref = rest[4]
    tiles = [tiles_ref[:, 128 * g : 128 * (g + 1)] for g in range(GRID)]
    block = block_of_lane(N)
    for m, entries in enumerate(RESULT):
        value = None
        for q, d in enumerate(entries):
            if d is None:
                continue
            g, p = place(d)
            part = tiles[g] if p == q else pltpu.roll(tiles[g], (32 * (q - p)) % 128, 1)
            value = part if value is None else jnp.where(block == q, part, value)
        result_ref[:, R * m : R * (m + 1), :] = value.reshape(8, R, 128)
    g, p = place(LAST)
    quarters = tiles[g].reshape(8, 4, 8, 128)
    block = block_of_lane(64)
    value = None
    for a in range(4):
        part = quarters[:, a].reshape(64, 128)
        part = part if a == p else pltpu.roll(part, (32 * (a - p)) % 128, 1)
        value = part if value is None else jnp.where(block == a, part, value)
    result_ref[:, OUT_ROWS - 8 :, :] = value.reshape(8, 8, 128)
    for k, out in zip(DISTANCES, outs):
        for e in range(2):
            out[e] = result_ref[target(k, e)]


def mirror_kernel(n_ref, mirror_ref, out_ref):
    out_ref[...] = n_ref[17:] + mirror_ref[...]


def join_kernel(n_ref, mirror_ref, *rest):
    received = rest[:4]
    other_ref, out_ref, r_scr, o_scr, sems = rest[4:]
    copies = [pltpu.make_async_copy(mirror_ref, out_ref.at[pl.ds(17, 15)], sems.at[17])]
    copies[0].start()
    for n, (k, ref) in enumerate(zip(DISTANCES, received)):
        r_scr[source(k, 0)] = ref[0]
        r_scr[source(k, 1)] = other_ref[n]
    halves = (slice(0, 128), slice(128, 256))

    def send_out(d):
        copies.append(pltpu.make_async_copy(o_scr.at[d], out_ref.at[d], sems.at[d]))
        copies[-1].start()

    for m, entries in enumerate(RESULT):
        for h, lanes in enumerate(halves):
            parts = [r_scr[4 * h + b, R * m : R * (m + 1)] for b in range(4)]
            for d, part in zip(entries, exchange_blocks(parts)):
                o_scr[d, :, lanes] = n_ref[d, :, lanes] + part
        for d in entries:
            send_out(d)
    for h, lanes in enumerate(halves):
        parts = [r_scr[4 * h + b, OUT_ROWS - 8 :] for b in range(4)]
        for a, part in enumerate(exchange_blocks(parts)):
            rows = slice(8 * a, 8 * (a + 1))
            o_scr[LAST, rows, lanes] = n_ref[LAST, rows, lanes] + part
    send_out(LAST)
    for copy in copies:
        copy.wait()


PARAMS = pltpu.CompilerParams(vmem_limit_bytes=24 * 1024 * 1024)
HBM = pl.BlockSpec(memory_space=pl.ANY)
SMEM = pl.BlockSpec(memory_space=pltpu.SMEM)
VMEM = pl.BlockSpec(memory_space=pltpu.VMEM)


def send(array, k, e):
    pairs = [(c, 2 * ((c // 2 + k) % 4) + (c + e) % 2) for c in range(8)]
    return lax.ppermute(array, "col", pairs)


def cost(units, elements):
    return pl.CostEstimate(flops=units * 18 * R * N * N, bytes_accessed=4 * elements, transcendentals=0)


def right_scratch(offsets):
    return [
        pltpu.VMEM((N, 9 * N), bf16),
        pltpu.VMEM((offsets * R, 3 * N), bf16),
        pltpu.VMEM((3, (offsets - 2) * R, N), f32),
    ]


def two_level(parts):
    parts = [part if k == 0 else send(part, k, 0) for k, part in zip(DISTANCES, parts)]
    return parts, send(jnp.stack([part[1] for part in parts]), 0, 1)


def body(noise_cov, couplings, shifts):
    edge, own = pl.pallas_call(
        edge_kernel,
        out_shape=[jax.ShapeDtypeStruct((HALO, R, N), f32), jax.ShapeDtypeStruct((23, R, N), f32)],
        in_specs=[VMEM],
        out_specs=[VMEM] * 2,
        compiler_params=PARAMS,
        cost_estimate=cost(200, 1 << 20),
        name="edge",
    )(noise_cov)
    halo = lax.ppermute(edge, "off", [(o, (o + 1) % 16) for o in range(16)])
    *local, first, taps = pl.pallas_call(
        local_kernel,
        out_shape=[jax.ShapeDtypeStruct((R, LOCAL_LANES), f32)] * 8 + [jax.ShapeDtypeStruct((HALO, R, N), f32), jax.ShapeDtypeStruct((3, N, N), f32)],
        in_specs=[SMEM, VMEM, VMEM],
        out_specs=[VMEM] * 10,
        scratch_shapes=right_scratch(23) + [pltpu.VMEM((8, R, LOCAL_LANES), f32)],
        compiler_params=PARAMS,
        cost_estimate=cost(57, 1 << 20),
        name="local_right_products",
    )(shifts, own, couplings)
    local = dict(zip(SLOTS, local))
    early = [send(local[slot], *slot) for slot in EARLY]
    halos = pl.pallas_call(
        halo_kernel,
        out_shape=[
            jax.ShapeDtypeStruct((R, HALO_LANES + LOCAL_LANES * (slot in LATE)), f32) for slot in SECOND
        ],
        in_specs=[VMEM] * 8,
        out_specs=[VMEM] * 8,
        scratch_shapes=right_scratch(12) + [pltpu.VMEM((8, R, HALO_LANES), f32)],
        compiler_params=PARAMS,
        cost_estimate=cost(10, 1 << 19),
        name="halo_right_products",
    )(halo, first, taps, *[local[slot] for slot in LATE])
    halos = [array if slot == (0, 0) else send(array, *slot) for array, slot in zip(halos, SECOND)]
    rows = pl.pallas_call(
        gather_kernel,
        out_shape=jax.ShapeDtypeStruct((N, LOCAL_LANES + HALO_LANES), f32),
        in_specs=[VMEM] * 11,
        out_specs=VMEM,
        compiler_params=PARAMS,
        cost_estimate=cost(10, 1 << 20),
        name="gather_rows",
    )(*early, local[0, 0], *halos)
    result, mirror = pl.pallas_call(
        left_kernel,
        out_shape=[jax.ShapeDtypeStruct((N, 128 * GRID), f32), jax.ShapeDtypeStruct((15, R, N), f32)],
        in_specs=[VMEM] * 2,
        out_specs=[VMEM] * 2,
        scratch_shapes=[
            pltpu.VMEM((N, 9 * N), bf16),
            pltpu.VMEM((9 * N, 128 * GRID), bf16),
        ],
        compiler_params=PARAMS,
        cost_estimate=cost(72, 1 << 21),
        name="left_products",
    )(taps, rows)
    rows = pl.pallas_call(
        pack_kernel,
        out_shape=[jax.ShapeDtypeStruct((2, OUT_ROWS, 128), f32)] * 4,
        in_specs=[VMEM],
        out_specs=[VMEM] * 4,
        scratch_shapes=[pltpu.VMEM((8, OUT_ROWS, 128), f32)],
        compiler_params=PARAMS,
        cost_estimate=cost(30, 1 << 19),
        name="pack",
    )(result)
    mirror = lax.ppermute(mirror, "off", [(o, 15 - o) for o in range(16)])
    mirror = pl.pallas_call(
        mirror_kernel,
        out_shape=jax.ShapeDtypeStruct((15, R, N), f32),
        in_specs=[VMEM] * 2,
        out_specs=VMEM,
        compiler_params=PARAMS,
        cost_estimate=cost(300, 1 << 19),
        name="join_mirror",
    )(noise_cov, mirror)
    rows, other = two_level(rows)
    return pl.pallas_call(
        join_kernel,
        out_shape=jax.ShapeDtypeStruct((R, R, N), f32),
        in_specs=[VMEM] * 7,
        out_specs=HBM,
        scratch_shapes=[
            pltpu.VMEM((8, OUT_ROWS, 128), f32),
            pltpu.VMEM((17, R, N), f32),
            pltpu.SemaphoreType.DMA((18,)),
        ],
        compiler_params=PARAMS,
        name="join",
    )(noise_cov, mirror, *rows, other)


def solution(mesh):
    return jax.shard_map(
        body,
        mesh=mesh,
        in_specs=(P("off", "col", None), P(), P()),
        out_specs=P("off", "col", None),
        check_vma=False,
    )
```

```python
import jax
import jax.numpy as jnp
from jax import lax
from jax.experimental import pallas as pl
from jax.experimental.pallas import tpu as pltpu
from jax.sharding import PartitionSpec as P

f32 = jnp.float32
bf16 = jnp.bfloat16

N = 256
R = 32
HALO = 6
GRID = 6
BASE = 3

def place(d):
    slot = d + BASE
    return slot % GRID, slot // GRID


def grid_tile(j, g, offsets):
    return [(j, GRID * q + g - BASE) if GRID * q + g - BASE in offsets else None for q in range(4)]


def local_tiles():
    tiles = [grid_tile(3, g, range(3, 20)) for g in range(GRID)]
    tiles += [grid_tile(2, g, range(2, 19)) for g in range(GRID)]
    tiles += [grid_tile(1, 5, range(1, 18))]
    free = [(tile, q) for tile in tiles[:-1] for q in range(4) if tile[q] is None]
    left = [d for d in range(1, 18) if place(d)[0] != 5]
    for tile, q in [f for f in free if f[1] == 3]:
        d = next(d for d in left if place(d)[1] == 3)
        left.remove(d)
        tile[q] = (1, d)
        free.remove((tile, q))
    for (tile, q), d in zip(free, left):
        tile[q] = (1, d)
    return tiles


LOCAL = local_tiles()
HALOS = [
    [(3, -3), (3, -2), (3, -1), (3, 0)],
    [(3, 1), (3, 2), (2, -2), (2, -1)],
    [(2, 0), (2, 1), (1, -1), (1, 0)],
]
WHERE = {entry: (m, p) for m, tile in enumerate(LOCAL + HALOS) for p, entry in enumerate(tile) if entry}
RESULT = [[5, 3, 9, 15], [11, 4, 10, 16], [0, 6, 12, 2], [1, 7, 13, 8]]
LAST = 14
DISTANCES = (0, 2, 1, 3)
OUT_ROWS = R * len(RESULT) + 8
LOCAL_LANES = 128 * len(LOCAL)
HALO_LANES = 128 * len(HALOS)
EARLY = [(2, 0), (2, 1)]
LATE = [(1, 0), (3, 0), (1, 1), (3, 1), (0, 1)]
SLOTS = EARLY + LATE + [(0, 0)]
SECOND = [(1, 0), (3, 0), (2, 0), (2, 1), (1, 1), (3, 1), (0, 1), (0, 0)]


def coordinates():
    col = lax.axis_index("col")
    return col // 2, col % 2


def target(k, e):
    z, core = coordinates()
    return 2 * ((z + k) % 4) + (core + e) % 2


def source(k, e):
    z, core = coordinates()
    return 2 * ((z + 4 - k) % 4) + (core + e) % 2


def split(x):
    high = x.astype(bf16)
    return high, (x - high.astype(f32)).astype(bf16)


def split_taps(c_ref, b_ref):
    for s in range(3):
        high, low = split(c_ref[s])
        k = 3 * N * s
        b_ref[:, k : k + N] = high
        b_ref[:, k + N : k + 2 * N] = high
        b_ref[:, k + 2 * N : k + 3 * N] = low


def block_of_lane(rows):
    return lax.broadcasted_iota(jnp.int32, (rows, 128), 1) // 32


def exchange_blocks(tiles):
    block = block_of_lane(tiles[0].shape[0])
    low = block < 2
    even = block % 2 == 0
    a = list(tiles)
    for q in (0, 1):
        x, y = a[q], a[q + 2]
        a[q] = jnp.where(low, x, pltpu.roll(y, 64, 1))
        a[q + 2] = jnp.where(low, pltpu.roll(x, 64, 1), y)
    for q in (0, 2):
        x, y = a[q], a[q + 1]
        a[q] = jnp.where(even, x, pltpu.roll(y, 32, 1))
        a[q + 1] = jnp.where(even, pltpu.roll(x, 96, 1), y)
    return a


def nt(x, y):
    return lax.dot_general(x, y, (((1,), (1,)), ((), ())), preferred_element_type=f32)


def nn(x, y):
    return lax.dot_general(x, y, (((1,), (0,)), ((), ())), preferred_element_type=f32)


def right_products(x, first, tiles, b_scr, x_scr, v_scr, m_ref):
    count = x.shape[0] // R
    start = {}
    for j in (1, 2, 3):
        high, low = split(x)
        x_scr[: count * R, :N] = high
        x_scr[: count * R, N : 2 * N] = low
        x_scr[: count * R, 2 * N :] = high
        count -= 2
        first += 1
        total = None
        for s in range(3):
            part = nt(x_scr[s * R : (s + count) * R], b_scr[:, 3 * N * s : 3 * N * (s + 1)])
            total = part if total is None else total + part
        x = total
        v_scr[j - 1, : count * R] = x
        start[j] = first
    for m, entries in enumerate(tiles):
        filler = next(entry for entry in entries if entry is not None)
        for h in range(2):
            parts = []
            for entry in entries:
                j, d = entry or filler
                row = (d - start[j]) * R
                parts.append(v_scr[j - 1, row : row + R, 128 * h : 128 * (h + 1)])
            for b, part in enumerate(exchange_blocks(parts)):
                m_ref[4 * h + b, :, 128 * m : 128 * (m + 1)] = part


def edge_kernel(n_ref, edge_ref, own_ref):
    edge_ref[...] = n_ref[R - HALO :]
    own_ref[...] = n_ref[:23]


def local_kernel(shift_ref, n_ref, c_ref, *rest):
    outs = rest[:8]
    first_ref, taps_ref, b_scr, x_scr, v_scr, m_scr = rest[8:]
    first_ref[...] = n_ref[:HALO]
    for s in (-1, 0, 1):
        block = None
        for t in range(3):
            chosen = jnp.where(shift_ref[t] == s, f32(1), f32(0)) * c_ref[t]
            block = chosen if block is None else block + chosen
        taps_ref[s + 1] = block
    split_taps(taps_ref, b_scr)
    right_products(n_ref[...].reshape(23 * R, N), 0, LOCAL, b_scr, x_scr, v_scr, m_scr)
    for out, slot in zip(outs, SLOTS):
        out[...] = m_scr[target(*slot)]


def halo_kernel(halo_ref, first_ref, c_ref, *rest):
    local = rest[:5]
    outs = rest[5:13]
    b_scr, x_scr, v_scr, m_scr = rest[13:]
    split_taps(c_ref, b_scr)
    x = jnp.concatenate([halo_ref[...].reshape(HALO * R, N), first_ref[...].reshape(HALO * R, N)], axis=0)
    right_products(x, -HALO, HALOS, b_scr, x_scr, v_scr, m_scr)
    for out, slot in zip(outs, SECOND):
        lane = 0
        if slot in LATE:
            lane = LOCAL_LANES
            out[:, :lane] = local[LATE.index(slot)][...]
        out[:, lane:] = m_scr[target(*slot)]


def gather_rows(refs, r_ref):
    local = dict(zip(EARLY + [(0, 0)], refs[:3]))
    for ref, slot in zip(refs[3:11], SECOND):
        rows = pl.ds(pl.multiple_of(source(*slot) * R, R), R)
        if slot in local:
            r_ref[rows, :LOCAL_LANES] = local[slot][...]
            r_ref[rows, LOCAL_LANES:] = ref[...]
        else:
            r_ref[rows, :] = ref[...]


def left_kernel(c_ref, *rest):
    tiles_ref, mirror_ref, r_ref, b_scr, x_scr = rest[11:]
    gather_rows(rest[:11], r_ref)
    split_taps(c_ref, b_scr)
    block = block_of_lane(N)
    total = None
    for j in (3, 2, 1):
        tiles = []
        for g in range(GRID):
            value = None
            for q in range(4):
                entry = (j, GRID * q + g - BASE)
                if entry not in WHERE:
                    continue
                m, p = WHERE[entry]
                part = r_ref[:, 128 * m : 128 * (m + 1)]
                if p != q:
                    part = pltpu.roll(part, (32 * (q - p)) % 128, 1)
                value = part if value is None else jnp.where(block == q, part, value)
            tiles.append(value if total is None else value + total[:, 128 * g : 128 * (g + 1)])
        edges = [pltpu.roll(tiles[-1], 32, 1)] + tiles + [pltpu.roll(tiles[0], 96, 1)]
        for g, part in enumerate(edges):
            high, low = split(part)
            for s in range(3):
                t = g - 2 + s
                if 0 <= t < GRID:
                    k = 3 * N * s
                    lanes = slice(128 * t, 128 * (t + 1))
                    x_scr[k : k + N, lanes] = high
                    x_scr[k + N : k + 2 * N, lanes] = low
                    x_scr[k + 2 * N : k + 3 * N, lanes] = high
        total = nn(b_scr[...], x_scr[...])
    tiles = [total[:, 128 * g : 128 * (g + 1)] for g in range(GRID)]
    for g in range(GRID):
        turned = tiles[g].T
        for q in range(4):
            d = GRID * q + g - BASE
            if 1 <= d <= 15:
                mirror_ref[15 - d] = turned[32 * q : 32 * (q + 1)]
    tiles_ref[...] = total


def pack_kernel(tiles_ref, *rest):
    outs = rest[:4]
    result_ref = rest[4]
    tiles = [tiles_ref[:, 128 * g : 128 * (g + 1)] for g in range(GRID)]
    block = block_of_lane(N)
    for m, entries in enumerate(RESULT):
        value = None
        for q, d in enumerate(entries):
            if d is None:
                continue
            g, p = place(d)
            part = tiles[g] if p == q else pltpu.roll(tiles[g], (32 * (q - p)) % 128, 1)
            value = part if value is None else jnp.where(block == q, part, value)
        result_ref[:, R * m : R * (m + 1), :] = value.reshape(8, R, 128)
    g, p = place(LAST)
    quarters = tiles[g].reshape(8, 4, 8, 128)
    block = block_of_lane(64)
    value = None
    for a in range(4):
        part = quarters[:, a].reshape(64, 128)
        part = part if a == p else pltpu.roll(part, (32 * (a - p)) % 128, 1)
        value = part if value is None else jnp.where(block == a, part, value)
    result_ref[:, OUT_ROWS - 8 :, :] = value.reshape(8, 8, 128)
    for k, out in zip(DISTANCES, outs):
        for e in range(2):
            out[e] = result_ref[target(k, e)]


def mirror_kernel(n_ref, mirror_ref, out_ref):
    out_ref[...] = n_ref[17:] + mirror_ref[...]


def join_kernel(n_ref, mirror_ref, *rest):
    received = rest[:4]
    other_ref, out_ref, r_scr, o_scr, sems = rest[4:]
    copies = [pltpu.make_async_copy(mirror_ref, out_ref.at[pl.ds(17, 15)], sems.at[17])]
    copies[0].start()
    for n, (k, ref) in enumerate(zip(DISTANCES, received)):
        r_scr[source(k, 0)] = ref[0]
        r_scr[source(k, 1)] = other_ref[n]
    halves = (slice(0, 128), slice(128, 256))

    def send_out(d):
        copies.append(pltpu.make_async_copy(o_scr.at[d], out_ref.at[d], sems.at[d]))
        copies[-1].start()

    for m, entries in enumerate(RESULT):
        for h, lanes in enumerate(halves):
            parts = [r_scr[4 * h + b, R * m : R * (m + 1)] for b in range(4)]
            for d, part in zip(entries, exchange_blocks(parts)):
                o_scr[d, :, lanes] = n_ref[d, :, lanes] + part
        for d in entries:
            send_out(d)
    for h, lanes in enumerate(halves):
        parts = [r_scr[4 * h + b, OUT_ROWS - 8 :] for b in range(4)]
        for a, part in enumerate(exchange_blocks(parts)):
            rows = slice(8 * a, 8 * (a + 1))
            o_scr[LAST, rows, lanes] = n_ref[LAST, rows, lanes] + part
    send_out(LAST)
    for copy in copies:
        copy.wait()


PARAMS = pltpu.CompilerParams(vmem_limit_bytes=24 * 1024 * 1024)
HBM = pl.BlockSpec(memory_space=pl.ANY)
SMEM = pl.BlockSpec(memory_space=pltpu.SMEM)
VMEM = pl.BlockSpec(memory_space=pltpu.VMEM)


def send(array, k, e):
    pairs = [(c, 2 * ((c // 2 + k) % 4) + (c + e) % 2) for c in range(8)]
    return lax.ppermute(array, "col", pairs)


def cost(units, elements):
    return pl.CostEstimate(flops=units * 18 * R * N * N, bytes_accessed=4 * elements, transcendentals=0)


def right_scratch(offsets):
    return [
        pltpu.VMEM((N, 9 * N), bf16),
        pltpu.VMEM((offsets * R, 3 * N), bf16),
        pltpu.VMEM((3, (offsets - 2) * R, N), f32),
    ]


def two_level(parts):
    parts = [part if k == 0 else send(part, k, 0) for k, part in zip(DISTANCES, parts)]
    return parts, send(jnp.stack([part[1] for part in parts]), 0, 1)


def body(noise_cov, couplings, shifts):
    edge, own = pl.pallas_call(
        edge_kernel,
        out_shape=[jax.ShapeDtypeStruct((HALO, R, N), f32), jax.ShapeDtypeStruct((23, R, N), f32)],
        in_specs=[VMEM],
        out_specs=[VMEM] * 2,
        compiler_params=PARAMS,
        cost_estimate=cost(200, 1 << 20),
        name="edge",
    )(noise_cov)
    halo = lax.ppermute(edge, "off", [(o, (o + 1) % 16) for o in range(16)])
    *local, first, taps = pl.pallas_call(
        local_kernel,
        out_shape=[jax.ShapeDtypeStruct((R, LOCAL_LANES), f32)] * 8 + [jax.ShapeDtypeStruct((HALO, R, N), f32), jax.ShapeDtypeStruct((3, N, N), f32)],
        in_specs=[SMEM, VMEM, VMEM],
        out_specs=[VMEM] * 10,
        scratch_shapes=right_scratch(23) + [pltpu.VMEM((8, R, LOCAL_LANES), f32)],
        compiler_params=PARAMS,
        cost_estimate=cost(57, 1 << 20),
        name="local_right_products",
    )(shifts, own, couplings)
    local = dict(zip(SLOTS, local))
    early = [send(local[slot], *slot) for slot in EARLY]
    halos = pl.pallas_call(
        halo_kernel,
        out_shape=[
            jax.ShapeDtypeStruct((R, HALO_LANES + LOCAL_LANES * (slot in LATE)), f32) for slot in SECOND
        ],
        in_specs=[VMEM] * 8,
        out_specs=[VMEM] * 8,
        scratch_shapes=right_scratch(12) + [pltpu.VMEM((8, R, HALO_LANES), f32)],
        compiler_params=PARAMS,
        cost_estimate=cost(10, 1 << 19),
        name="halo_right_products",
    )(halo, first, taps, *[local[slot] for slot in LATE])
    halos = [array if slot == (0, 0) else send(array, *slot) for array, slot in zip(halos, SECOND)]
    result, mirror = pl.pallas_call(
        left_kernel,
        out_shape=[jax.ShapeDtypeStruct((N, 128 * GRID), f32), jax.ShapeDtypeStruct((15, R, N), f32)],
        in_specs=[VMEM] * 12,
        out_specs=[VMEM] * 2,
        scratch_shapes=[
            pltpu.VMEM((N, LOCAL_LANES + HALO_LANES), f32),
            pltpu.VMEM((N, 9 * N), bf16),
            pltpu.VMEM((9 * N, 128 * GRID), bf16),
        ],
        compiler_params=PARAMS,
        cost_estimate=cost(72, 1 << 21),
        name="left_products",
    )(taps, *early, local[0, 0], *halos)
    rows = pl.pallas_call(
        pack_kernel,
        out_shape=[jax.ShapeDtypeStruct((2, OUT_ROWS, 128), f32)] * 4,
        in_specs=[VMEM],
        out_specs=[VMEM] * 4,
        scratch_shapes=[pltpu.VMEM((8, OUT_ROWS, 128), f32)],
        compiler_params=PARAMS,
        cost_estimate=cost(30, 1 << 19),
        name="pack",
    )(result)
    mirror = lax.ppermute(mirror, "off", [(o, 15 - o) for o in range(16)])
    mirror = pl.pallas_call(
        mirror_kernel,
        out_shape=jax.ShapeDtypeStruct((15, R, N), f32),
        in_specs=[VMEM] * 2,
        out_specs=VMEM,
        compiler_params=PARAMS,
        cost_estimate=cost(300, 1 << 19),
        name="join_mirror",
    )(noise_cov, mirror)
    rows, other = two_level(rows)
    return pl.pallas_call(
        join_kernel,
        out_shape=jax.ShapeDtypeStruct((R, R, N), f32),
        in_specs=[VMEM] * 7,
        out_specs=HBM,
        scratch_shapes=[
            pltpu.VMEM((8, OUT_ROWS, 128), f32),
            pltpu.VMEM((17, R, N), f32),
            pltpu.SemaphoreType.DMA((18,)),
        ],
        compiler_params=PARAMS,
        name="join",
    )(noise_cov, mirror, *rows, other)


def solution(mesh):
    return jax.shard_map(
        body,
        mesh=mesh,
        in_specs=(P("off", "col", None), P(), P()),
        out_specs=P("off", "col", None),
        check_vma=False,
    )
```

```python
import jax
import jax.numpy as jnp
from jax import lax
from jax.experimental import pallas as pl
from jax.experimental.pallas import tpu as pltpu
from jax.sharding import PartitionSpec as P

f32 = jnp.float32
bf16 = jnp.bfloat16

N = 256
R = 32
HALO = 6
GRID = 6
BASE = 3

def place(d):
    slot = d + BASE
    return slot % GRID, slot // GRID


def grid_tile(j, g, offsets):
    return [(j, GRID * q + g - BASE) if GRID * q + g - BASE in offsets else None for q in range(4)]


def local_tiles():
    tiles = [grid_tile(3, g, range(3, 20)) for g in range(GRID)]
    tiles += [grid_tile(2, g, range(2, 19)) for g in range(GRID)]
    tiles += [grid_tile(1, 5, range(1, 18))]
    free = [(tile, q) for tile in tiles[:-1] for q in range(4) if tile[q] is None]
    left = [d for d in range(1, 18) if place(d)[0] != 5]
    for tile, q in [f for f in free if f[1] == 3]:
        d = next(d for d in left if place(d)[1] == 3)
        left.remove(d)
        tile[q] = (1, d)
        free.remove((tile, q))
    for (tile, q), d in zip(free, left):
        tile[q] = (1, d)
    return tiles


LOCAL = local_tiles()
HALOS = [
    [(3, -3), (3, -2), (3, -1), (3, 0)],
    [(3, 1), (3, 2), (2, -2), (2, -1)],
    [(2, 0), (2, 1), (1, -1), (1, 0)],
]
WHERE = {entry: (m, p) for m, tile in enumerate(LOCAL + HALOS) for p, entry in enumerate(tile) if entry}
RESULT = [[5, 3, 9, 15], [11, 4, 10, 16], [0, 6, 12, 2], [1, 7, 13, 8]]
LAST = 14
DISTANCES = (0, 1, 3, 2)
OUT_ROWS = R * len(RESULT) + 8
LOCAL_LANES = 128 * len(LOCAL)
HALO_LANES = 128 * len(HALOS)
EARLY = [(2, 0), (2, 1)]
LATE = [(1, 0), (3, 0), (1, 1), (3, 1), (0, 1)]
SLOTS = EARLY + LATE + [(0, 0)]
SECOND = [(1, 0), (3, 0), (2, 0), (2, 1), (1, 1), (3, 1), (0, 1), (0, 0)]


def coordinates():
    col = lax.axis_index("col")
    return col // 2, col % 2


def target(k, e):
    z, core = coordinates()
    return 2 * ((z + k) % 4) + (core + e) % 2


def source(k, e):
    z, core = coordinates()
    return 2 * ((z + 4 - k) % 4) + (core + e) % 2


def split(x):
    high = x.astype(bf16)
    return high, (x - high.astype(f32)).astype(bf16)


def split_taps(c_ref, b_ref):
    for s in range(3):
        high, low = split(c_ref[s])
        k = 3 * N * s
        b_ref[:, k : k + N] = high
        b_ref[:, k + N : k + 2 * N] = high
        b_ref[:, k + 2 * N : k + 3 * N] = low


def block_of_lane(rows):
    return lax.broadcasted_iota(jnp.int32, (rows, 128), 1) // 32


def exchange_blocks(tiles):
    block = block_of_lane(tiles[0].shape[0])
    low = block < 2
    even = block % 2 == 0
    a = list(tiles)
    for q in (0, 1):
        x, y = a[q], a[q + 2]
        a[q] = jnp.where(low, x, pltpu.roll(y, 64, 1))
        a[q + 2] = jnp.where(low, pltpu.roll(x, 64, 1), y)
    for q in (0, 2):
        x, y = a[q], a[q + 1]
        a[q] = jnp.where(even, x, pltpu.roll(y, 32, 1))
        a[q + 1] = jnp.where(even, pltpu.roll(x, 96, 1), y)
    return a


def nt(x, y):
    return lax.dot_general(x, y, (((1,), (1,)), ((), ())), preferred_element_type=f32)


def nn(x, y):
    return lax.dot_general(x, y, (((1,), (0,)), ((), ())), preferred_element_type=f32)


def right_products(x, first, tiles, b_scr, x_scr, v_scr, m_ref):
    count = x.shape[0] // R
    start = {}
    for j in (1, 2, 3):
        high, low = split(x)
        x_scr[: count * R, :N] = high
        x_scr[: count * R, N : 2 * N] = low
        x_scr[: count * R, 2 * N :] = high
        count -= 2
        first += 1
        total = None
        for s in range(3):
            part = nt(x_scr[s * R : (s + count) * R], b_scr[:, 3 * N * s : 3 * N * (s + 1)])
            total = part if total is None else total + part
        x = total
        v_scr[j - 1, : count * R] = x
        start[j] = first
    for m, entries in enumerate(tiles):
        filler = next(entry for entry in entries if entry is not None)
        for h in range(2):
            parts = []
            for entry in entries:
                j, d = entry or filler
                row = (d - start[j]) * R
                parts.append(v_scr[j - 1, row : row + R, 128 * h : 128 * (h + 1)])
            for b, part in enumerate(exchange_blocks(parts)):
                m_ref[4 * h + b, :, 128 * m : 128 * (m + 1)] = part


def edge_kernel(n_ref, edge_ref, own_ref):
    edge_ref[...] = n_ref[R - HALO :]
    own_ref[...] = n_ref[:23]


def local_kernel(shift_ref, n_ref, c_ref, *rest):
    outs = rest[:8]
    first_ref, taps_ref, b_scr, x_scr, v_scr, m_scr = rest[8:]
    first_ref[...] = n_ref[:HALO]
    for s in (-1, 0, 1):
        block = None
        for t in range(3):
            chosen = jnp.where(shift_ref[t] == s, f32(1), f32(0)) * c_ref[t]
            block = chosen if block is None else block + chosen
        taps_ref[s + 1] = block
    split_taps(taps_ref, b_scr)
    right_products(n_ref[...].reshape(23 * R, N), 0, LOCAL, b_scr, x_scr, v_scr, m_scr)
    for out, slot in zip(outs, SLOTS):
        out[...] = m_scr[target(*slot)]


def halo_kernel(halo_ref, first_ref, c_ref, *rest):
    local = rest[:5]
    outs = rest[5:13]
    b_scr, x_scr, v_scr, m_scr = rest[13:]
    split_taps(c_ref, b_scr)
    x = jnp.concatenate([halo_ref[...].reshape(HALO * R, N), first_ref[...].reshape(HALO * R, N)], axis=0)
    right_products(x, -HALO, HALOS, b_scr, x_scr, v_scr, m_scr)
    for out, slot in zip(outs, SECOND):
        lane = 0
        if slot in LATE:
            lane = LOCAL_LANES
            out[:, :lane] = local[LATE.index(slot)][...]
        out[:, lane:] = m_scr[target(*slot)]


def gather_rows(refs, r_ref):
    local = dict(zip(EARLY + [(0, 0)], refs[:3]))
    for ref, slot in zip(refs[3:11], SECOND):
        rows = pl.ds(pl.multiple_of(source(*slot) * R, R), R)
        if slot in local:
            r_ref[rows, :LOCAL_LANES] = local[slot][...]
            r_ref[rows, LOCAL_LANES:] = ref[...]
        else:
            r_ref[rows, :] = ref[...]


def left_kernel(c_ref, *rest):
    tiles_ref, mirror_ref, r_ref, b_scr, x_scr = rest[11:]
    gather_rows(rest[:11], r_ref)
    split_taps(c_ref, b_scr)
    block = block_of_lane(N)
    total = None
    for j in (3, 2, 1):
        tiles = []
        for g in range(GRID):
            value = None
            for q in range(4):
                entry = (j, GRID * q + g - BASE)
                if entry not in WHERE:
                    continue
                m, p = WHERE[entry]
                part = r_ref[:, 128 * m : 128 * (m + 1)]
                if p != q:
                    part = pltpu.roll(part, (32 * (q - p)) % 128, 1)
                value = part if value is None else jnp.where(block == q, part, value)
            tiles.append(value if total is None else value + total[:, 128 * g : 128 * (g + 1)])
        edges = [pltpu.roll(tiles[-1], 32, 1)] + tiles + [pltpu.roll(tiles[0], 96, 1)]
        for g, part in enumerate(edges):
            high, low = split(part)
            for s in range(3):
                t = g - 2 + s
                if 0 <= t < GRID:
                    k = 3 * N * s
                    lanes = slice(128 * t, 128 * (t + 1))
                    x_scr[k : k + N, lanes] = high
                    x_scr[k + N : k + 2 * N, lanes] = low
                    x_scr[k + 2 * N : k + 3 * N, lanes] = high
        total = nn(b_scr[...], x_scr[...])
    tiles = [total[:, 128 * g : 128 * (g + 1)] for g in range(GRID)]
    for g in range(GRID):
        turned = tiles[g].T
        for q in range(4):
            d = GRID * q + g - BASE
            if 1 <= d <= 15:
                mirror_ref[15 - d] = turned[32 * q : 32 * (q + 1)]
    tiles_ref[...] = total


def pack_kernel(tiles_ref, *rest):
    outs = rest[:4]
    result_ref = rest[4]
    tiles = [tiles_ref[:, 128 * g : 128 * (g + 1)] for g in range(GRID)]
    block = block_of_lane(N)
    for m, entries in enumerate(RESULT):
        value = None
        for q, d in enumerate(entries):
            if d is None:
                continue
            g, p = place(d)
            part = tiles[g] if p == q else pltpu.roll(tiles[g], (32 * (q - p)) % 128, 1)
            value = part if value is None else jnp.where(block == q, part, value)
        result_ref[:, R * m : R * (m + 1), :] = value.reshape(8, R, 128)
    g, p = place(LAST)
    quarters = tiles[g].reshape(8, 4, 8, 128)
    block = block_of_lane(64)
    value = None
    for a in range(4):
        part = quarters[:, a].reshape(64, 128)
        part = part if a == p else pltpu.roll(part, (32 * (a - p)) % 128, 1)
        value = part if value is None else jnp.where(block == a, part, value)
    result_ref[:, OUT_ROWS - 8 :, :] = value.reshape(8, 8, 128)
    for k, out in zip(DISTANCES, outs):
        for e in range(2):
            out[e] = result_ref[target(k, e)]


def mirror_kernel(n_ref, mirror_ref, out_ref):
    out_ref[...] = n_ref[17:] + mirror_ref[...]


def join_kernel(n_ref, mirror_ref, *rest):
    received = rest[:4]
    other_ref, out_ref, r_scr, o_scr, sems = rest[4:]
    copies = [pltpu.make_async_copy(mirror_ref, out_ref.at[pl.ds(17, 15)], sems.at[17])]
    copies[0].start()
    for n, (k, ref) in enumerate(zip(DISTANCES, received)):
        r_scr[source(k, 0)] = ref[0]
        r_scr[source(k, 1)] = other_ref[n]
    halves = (slice(0, 128), slice(128, 256))

    def send_out(d):
        copies.append(pltpu.make_async_copy(o_scr.at[d], out_ref.at[d], sems.at[d]))
        copies[-1].start()

    for m, entries in enumerate(RESULT):
        for h, lanes in enumerate(halves):
            parts = [r_scr[4 * h + b, R * m : R * (m + 1)] for b in range(4)]
            for d, part in zip(entries, exchange_blocks(parts)):
                o_scr[d, :, lanes] = n_ref[d, :, lanes] + part
        for d in entries:
            send_out(d)
    for h, lanes in enumerate(halves):
        parts = [r_scr[4 * h + b, OUT_ROWS - 8 :] for b in range(4)]
        for a, part in enumerate(exchange_blocks(parts)):
            rows = slice(8 * a, 8 * (a + 1))
            o_scr[LAST, rows, lanes] = n_ref[LAST, rows, lanes] + part
    send_out(LAST)
    for copy in copies:
        copy.wait()


PARAMS = pltpu.CompilerParams(vmem_limit_bytes=24 * 1024 * 1024)
HBM = pl.BlockSpec(memory_space=pl.ANY)
SMEM = pl.BlockSpec(memory_space=pltpu.SMEM)
VMEM = pl.BlockSpec(memory_space=pltpu.VMEM)


def send(array, k, e):
    pairs = [(c, 2 * ((c // 2 + k) % 4) + (c + e) % 2) for c in range(8)]
    return lax.ppermute(array, "col", pairs)


def cost(units, elements):
    return pl.CostEstimate(flops=units * 18 * R * N * N, bytes_accessed=4 * elements, transcendentals=0)


def right_scratch(offsets):
    return [
        pltpu.VMEM((N, 9 * N), bf16),
        pltpu.VMEM((offsets * R, 3 * N), bf16),
        pltpu.VMEM((3, (offsets - 2) * R, N), f32),
    ]


def two_level(parts):
    parts = [part if k == 0 else send(part, k, 0) for k, part in zip(DISTANCES, parts)]
    return parts, send(jnp.stack([part[1] for part in parts]), 0, 1)


def body(noise_cov, couplings, shifts):
    edge, own = pl.pallas_call(
        edge_kernel,
        out_shape=[jax.ShapeDtypeStruct((HALO, R, N), f32), jax.ShapeDtypeStruct((23, R, N), f32)],
        in_specs=[VMEM],
        out_specs=[VMEM] * 2,
        compiler_params=PARAMS,
        cost_estimate=cost(200, 1 << 20),
        name="edge",
    )(noise_cov)
    halo = lax.ppermute(edge, "off", [(o, (o + 1) % 16) for o in range(16)])
    *local, first, taps = pl.pallas_call(
        local_kernel,
        out_shape=[jax.ShapeDtypeStruct((R, LOCAL_LANES), f32)] * 8 + [jax.ShapeDtypeStruct((HALO, R, N), f32), jax.ShapeDtypeStruct((3, N, N), f32)],
        in_specs=[SMEM, VMEM, VMEM],
        out_specs=[VMEM] * 10,
        scratch_shapes=right_scratch(23) + [pltpu.VMEM((8, R, LOCAL_LANES), f32)],
        compiler_params=PARAMS,
        cost_estimate=cost(57, 1 << 20),
        name="local_right_products",
    )(shifts, own, couplings)
    local = dict(zip(SLOTS, local))
    early = [send(local[slot], *slot) for slot in EARLY]
    halos = pl.pallas_call(
        halo_kernel,
        out_shape=[
            jax.ShapeDtypeStruct((R, HALO_LANES + LOCAL_LANES * (slot in LATE)), f32) for slot in SECOND
        ],
        in_specs=[VMEM] * 8,
        out_specs=[VMEM] * 8,
        scratch_shapes=right_scratch(12) + [pltpu.VMEM((8, R, HALO_LANES), f32)],
        compiler_params=PARAMS,
        cost_estimate=cost(10, 1 << 19),
        name="halo_right_products",
    )(halo, first, taps, *[local[slot] for slot in LATE])
    halos = [array if slot == (0, 0) else send(array, *slot) for array, slot in zip(halos, SECOND)]
    result, mirror = pl.pallas_call(
        left_kernel,
        out_shape=[jax.ShapeDtypeStruct((N, 128 * GRID), f32), jax.ShapeDtypeStruct((15, R, N), f32)],
        in_specs=[VMEM] * 12,
        out_specs=[VMEM] * 2,
        scratch_shapes=[
            pltpu.VMEM((N, LOCAL_LANES + HALO_LANES), f32),
            pltpu.VMEM((N, 9 * N), bf16),
            pltpu.VMEM((9 * N, 128 * GRID), bf16),
        ],
        compiler_params=PARAMS,
        cost_estimate=cost(72, 1 << 21),
        name="left_products",
    )(taps, *early, local[0, 0], *halos)
    rows = pl.pallas_call(
        pack_kernel,
        out_shape=[jax.ShapeDtypeStruct((2, OUT_ROWS, 128), f32)] * 4,
        in_specs=[VMEM],
        out_specs=[VMEM] * 4,
        scratch_shapes=[pltpu.VMEM((8, OUT_ROWS, 128), f32)],
        compiler_params=PARAMS,
        cost_estimate=cost(30, 1 << 19),
        name="pack",
    )(result)
    mirror = lax.ppermute(mirror, "off", [(o, 15 - o) for o in range(16)])
    mirror = pl.pallas_call(
        mirror_kernel,
        out_shape=jax.ShapeDtypeStruct((15, R, N), f32),
        in_specs=[VMEM] * 2,
        out_specs=VMEM,
        compiler_params=PARAMS,
        cost_estimate=cost(300, 1 << 19),
        name="join_mirror",
    )(noise_cov, mirror)
    rows, other = two_level(rows)
    return pl.pallas_call(
        join_kernel,
        out_shape=jax.ShapeDtypeStruct((R, R, N), f32),
        in_specs=[VMEM] * 7,
        out_specs=HBM,
        scratch_shapes=[
            pltpu.VMEM((8, OUT_ROWS, 128), f32),
            pltpu.VMEM((17, R, N), f32),
            pltpu.SemaphoreType.DMA((18,)),
        ],
        compiler_params=PARAMS,
        name="join",
    )(noise_cov, mirror, *rows, other)


def solution(mesh):
    return jax.shard_map(
        body,
        mesh=mesh,
        in_specs=(P("off", "col", None), P(), P()),
        out_specs=P("off", "col", None),
        check_vma=False,
    )
```
